512 devices in a mesh: grp: 16 (over z_lo, core), xy: 32 (over x, y, z_hi).
Axes of the slice: x: 4, y: 4, z: 16 (z_hi: 2, z_lo: 8; z = z_hi * 8 + z_lo), core: 2. Of those that a mesh axis runs over, the one named last changes fastest.
Arguments:
- activations: bfloat16 [64, 512, 32, 128], P(None, ('grp', 'xy')), may hold values from -6 to 6
- cotangent: bfloat16 [64, 64, 32, 128], P(None, 'grp', 'xy'), may hold values from -6 to 6
- weight: bfloat16 [9, 64, 64], replicated, may hold values from -0.25 to 0.25
- conv_bias: float32 [64], replicated, may hold values from -3 to 3
- blur_taps: float32 [9], replicated, may hold values from 0.1 to 1
Outputs:
- grad_input: bfloat16 [64, 512, 32, 128], P(None, ('grp', 'xy'))
- grad_weight: float32 [9, 64, 64], replicated
- grad_bias: float32 [64], replicated
The draws below stay inside these ranges and needn't reach their ends.
All inputs are finite; a program needn't handle non-finite values.
Results may differ from the reference program's by a relative error of at most 0.0052.
Values may be sent and summed in bfloat16 or wider, within the bound.
No kernel may reach another device: no remote copies, remote signals or barrier semaphores. Data moves between devices by JAX's collectives and lax.ppermute only.
A program may use at most 64 MiB of HBM per device.

```python
import math
import jax
import jax.numpy as jnp
from jax import lax

C = 64
R = 8
SLAB = 1
Y = 32
X = 128
KZ = 9
Z = 512
ZL = 64
N_XY = 32


def levels(rng, shape, pieces, low, top_value):
    level, own = 1.0, jax.random.fold_in(rng, 6)
    for position, parts in pieces:
        heights = jnp.exp(jax.random.uniform(jax.random.fold_in(own, position), (parts,), jnp.float32, low / len(pieces), top_value / len(pieces)))
        level = level * jnp.repeat(heights, shape[position] // parts).reshape([-1 if axis == position else 1 for axis in range(len(shape))])
    return level


def scatter_about(key, extent, scale, bound, cuts=(), held_as=jnp.bfloat16):
    values = jax.random.normal(key, extent, jnp.float32) * scale
    if len(cuts) > 0:
        values = levels(key, extent, cuts, -0.22, 0.18) * values
    return jnp.clip(values, min=-bound, max=bound).astype(held_as)


def setup_inputs(seed: int = 0) -> dict:
    key_of = jax.random.split(jax.random.key(seed), 6)
    activations = scatter_about(key_of[0], (C, Z, Y, X), 1.0, 6.0, ((1, 512),))
    cotangent = scatter_about(key_of[1], (C, ZL, Y, X), 1.0, 6.0, ((1, 16), (2, 32)))
    weight = scatter_about(key_of[2], (9, C, C), (9 * C) ** -0.5, 0.25)
    conv_bias = scatter_about(key_of[3], (C,), 0.5, 3.0, (), jnp.float32)
    blur_taps = jnp.clip(jnp.exp(jax.random.uniform(key_of[4], (KZ,), jnp.float32, math.log(0.1), math.log(1.0))), 0.1, 1.0)
    return {"activations": activations, "cotangent": cotangent, "weight": weight, "conv_bias": conv_bias, "blur_taps": blur_taps}


def upsample_adjoint(channel, blur_taps):
    inserted = jnp.zeros((ZL, R, Y, X), jnp.float32).at[:, R // 2].set(channel.astype(jnp.float32))
    spread = inserted.reshape(Z, Y, X)
    half_taps = R // 2
    padded = jnp.pad(spread, ((half_taps, half_taps), (0, 0), (0, 0)))
    summed = jnp.zeros((Z, Y, X), jnp.float32)
    for offset in range(2 * half_taps + 1):
        start = 2 * half_taps - offset
        summed = summed + blur_taps[offset] * padded[start:start + Z]
    return summed.astype(jnp.bfloat16)


def forward_taps(volume, weight):
    channels, planes, rows, cols = volume.shape
    padded = jnp.pad(volume, ((0, 0), (0, 0), (1, 1), (1, 1)))
    summed = jnp.zeros((channels, planes * rows * cols), jnp.float32)
    for offset in range(9):
        row_off = offset // 3
        col_off = offset % 3
        shifted = padded[:, :, row_off:row_off + rows, col_off:col_off + cols].reshape(channels, -1)
        summed = summed + jnp.dot(weight[offset], shifted, preferred_element_type=jnp.float32)
    return summed


def backward_taps(volume, grad_hidden, weight):
    channels, planes, rows, cols = volume.shape
    padded_in = jnp.pad(volume, ((0, 0), (0, 0), (1, 1), (1, 1)))
    padded_grad = jnp.pad(grad_hidden, ((0, 0), (0, 0), (1, 1), (1, 1)))
    grad_flat = grad_hidden.reshape(channels, -1)
    summed = jnp.zeros((channels, planes * rows * cols), jnp.float32)
    grad_list = []
    for offset in range(9):
        row_off = offset // 3
        col_off = offset % 3
        shifted_in = padded_in[:, :, row_off:row_off + rows, col_off:col_off + cols].reshape(channels, -1)
        grad_list.append(lax.dot_general(grad_flat, shifted_in, (((1,), (1,)), ((), ())), preferred_element_type=jnp.float32))
        shifted_grad = padded_grad[:, :, 2 - row_off:2 - row_off + rows, 2 - col_off:2 - col_off + cols].reshape(channels, -1)
        summed = summed + jnp.dot(weight[offset].T, shifted_grad, preferred_element_type=jnp.float32)
    return jnp.stack(grad_list, 0), summed


def layer_backward(volume, g_out, weight, conv_bias):
    channels = volume.shape[0]
    hidden = forward_taps(volume, weight) + conv_bias[:, None]
    sigmoid_h = jax.nn.sigmoid(hidden)
    slope_h = sigmoid_h * (1.0 + hidden * (1.0 - sigmoid_h))
    grad_flat = g_out.reshape(channels, -1).astype(jnp.float32)
    grad_hidden = (grad_flat * slope_h).astype(jnp.bfloat16)
    grad_w, grad_conv = backward_taps(volume, grad_hidden.reshape(volume.shape), weight)
    grad_bias = jnp.sum(grad_hidden.astype(jnp.float32), axis=1)
    grad_input = (grad_flat + grad_conv).reshape(volume.shape).astype(jnp.bfloat16)
    return grad_input, grad_w, grad_bias


def reference(activations, cotangent, weight, conv_bias, blur_taps):
    g_out = lax.map(lambda channel: upsample_adjoint(channel, blur_taps), cotangent)
    group_depth = SLAB * N_XY
    group_count = Z // group_depth
    act_blocks = activations.reshape(C, group_count, group_depth, Y, X).transpose(1, 0, 2, 3, 4)
    grad_blocks = g_out.reshape(C, group_count, group_depth, Y, X).transpose(1, 0, 2, 3, 4)
    grad_input, grad_w, grad_bias = lax.map(lambda paired: layer_backward(paired[0], paired[1], weight, conv_bias), (act_blocks, grad_blocks))
    grad_input = grad_input.transpose(1, 0, 2, 3, 4).reshape(C, Z, Y, X)
    factor = float(Z * Y * X) ** -0.5
    return grad_input, jnp.sum(grad_w, 0) * factor, jnp.sum(grad_bias, 0) * factor
```

```python
import jax
import jax.numpy as jnp
from jax import lax
from jax.experimental import pallas as pl
from jax.experimental.pallas import tpu as pltpu
from jax.sharding import Mesh
from jax.sharding import PartitionSpec as P

R = 8
C = 64
Y = 32
X = 128
AXES = ("zl", "core", "x", "y", "zh")
SIZES = (8, 2, 4, 4, 2)
GROUP = ("zl", "core")
PLANE = ("x", "y", "zh")
FLAT = ("core", "x", "y")
COLUMN = ("zl", "zh")
N_FLAT = 32
N_COLUMN = 16
PIECE = 8
WIDE = 256
VMEM_LIMIT = 48 * 1024 * 1024


def shifted(row, step):
    if step == 0:
        return row
    lane = lax.broadcasted_iota(jnp.int32, row.shape, 1)
    edge = 0 if step < 0 else X - 1
    return jnp.where(lane == edge, 0.0, pltpu.roll(row, (-step) % X, 1))


def forward_kernel(act_ref, mix_ref, bias_ref, slope_ref, turned_ref, stack, hidden):
    column = lax.broadcasted_iota(jnp.int32, (X, WIDE - 3 * C), 1)
    ones = jnp.where(column == 0, 1.0, 0.0).astype(jnp.bfloat16)

    def spread(y, carry):
        row = act_ref[y].astype(jnp.float32)
        at = pl.ds(pl.multiple_of(y * X, X), X)
        whole = jnp.concatenate([shifted(row, b - 1) for b in range(3)], axis=0)
        stack[:, at] = whole.astype(jnp.bfloat16)
        turned_ref[at, : 3 * C] = whole.T.astype(jnp.bfloat16)
        turned_ref[at, 3 * C :] = ones
        return carry

    lax.fori_loop(0, Y, spread, 0)
    hidden[...] = jnp.broadcast_to(bias_ref[...], hidden.shape)

    def taps(j, carry):
        at = pl.multiple_of(j * 2 * X, 2 * X)
        part = jnp.dot(
            mix_ref[...], stack[:, pl.ds(at, 2 * X)], preferred_element_type=jnp.float32
        )
        for a in range(3):
            place = pl.ds(pl.multiple_of(at + (2 - a) * X, X), 2 * X)
            hidden[:, place] += part[a * C : (a + 1) * C]
        return carry

    lax.fori_loop(0, Y // 2, taps, 0)

    def slopes(y, carry):
        h = hidden[:, pl.ds(pl.multiple_of((y + 1) * X, X), X)]
        s = jax.nn.sigmoid(h)
        slope_ref[y] = s * (1.0 + h * (1.0 - s))
        return carry

    lax.fori_loop(0, Y, slopes, 0)


def weight_kernel(g_ref, slope_ref, turned_ref, grad_ref, sums_ref, stack):
    zero = jnp.zeros((C, X), jnp.bfloat16)
    stack[0:C, (Y - 1) * X :] = zero
    stack[2 * C :, 0:X] = zero
    for y in range(Y):
        grad = (g_ref[y].astype(jnp.float32) * slope_ref[y]).astype(jnp.bfloat16)
        grad_ref[y] = grad
        for a in range(3):
            row = y + a - 1
            if 0 <= row < Y:
                stack[a * C : (a + 1) * C, row * X : (row + 1) * X] = grad
    total = jnp.zeros((3 * C, WIDE), jnp.float32)
    for j in range(Y // 2):
        at = slice(j * 2 * X, (j + 1) * 2 * X)
        total += jnp.dot(stack[:, at], turned_ref[at, :], preferred_element_type=jnp.float32)
    sums_ref[: 3 * C // PIECE] = total.reshape(3 * C // PIECE, PIECE, WIDE)
    bias = total[C : 2 * C, 3 * C : 3 * C + 1]
    diagonal = lax.broadcasted_iota(jnp.int32, (C, WIDE), 0) == lax.broadcasted_iota(
        jnp.int32, (C, WIDE), 1
    )
    row = jnp.sum(jnp.where(diagonal, bias, 0.0), axis=0, keepdims=True)
    first = lax.broadcasted_iota(jnp.int32, (PIECE, WIDE), 0) == 0
    sums_ref[3 * C // PIECE] = jnp.where(first, row, 0.0)
    sums_ref[3 * C // PIECE + 1 :] = jnp.zeros(
        (N_FLAT - 3 * C // PIECE - 1, PIECE, WIDE), jnp.float32
    )


def input_kernel(grad_ref, g_ref, mix_ref, out_ref, stack, total):
    total[...] = jnp.zeros_like(total)

    def spread(y, carry):
        row = grad_ref[y].astype(jnp.float32)
        at = pl.ds(pl.multiple_of(y * X, X), X)
        whole = jnp.concatenate([shifted(row, 1 - b) for b in range(3)], axis=0)
        stack[:, at] = whole.astype(jnp.bfloat16)
        return carry

    lax.fori_loop(0, Y, spread, 0)

    def taps(j, carry):
        at = pl.multiple_of(j * 2 * X, 2 * X)
        part = jnp.dot(
            mix_ref[...], stack[:, pl.ds(at, 2 * X)], preferred_element_type=jnp.float32
        )
        for a in range(3):
            place = pl.ds(pl.multiple_of(at + a * X, X), 2 * X)
            total[:, place] += part[a * C : (a + 1) * C]
        return carry

    lax.fori_loop(0, Y // 2, taps, 0)

    def finish(y, carry):
        conv = total[:, pl.ds(pl.multiple_of((y + 1) * X, X), X)]
        out_ref[y] = (g_ref[y].astype(jnp.float32) + conv).astype(jnp.bfloat16)
        return carry

    lax.fori_loop(0, Y, finish, 0)


def spread_sum_kernel(parts_ref, out_ref):
    total = jnp.sum(parts_ref[...], axis=0)
    for copy in range(out_ref.shape[0]):
        out_ref[copy] = total


def scaled_sum_kernel(factor, parts_ref, out_ref):
    total = jnp.sum(parts_ref[...], axis=0) * factor
    for copy in range(out_ref.shape[0]):
        out_ref[copy] = total


def call(kernel, outs, scratch, flops, moved, *args):
    return pl.pallas_call(
        kernel,
        out_shape=outs,
        in_specs=[pl.BlockSpec(memory_space=pltpu.VMEM)] * len(args),
        out_specs=jax.tree.map(lambda _: pl.BlockSpec(memory_space=pltpu.VMEM), outs),
        scratch_shapes=scratch,
        compiler_params=pltpu.CompilerParams(vmem_limit_bytes=VMEM_LIMIT),
        cost_estimate=pl.CostEstimate(flops=flops, bytes_accessed=moved, transcendentals=0),
    )(*args)


def on_device(activations, cotangent, weight, conv_bias, blur_taps):
    shape = jax.ShapeDtypeStruct
    bf16, f32 = jnp.bfloat16, jnp.float32
    groups = 16
    coarse = cotangent[:, :, 0, :].transpose(1, 0, 2)
    hops = [(g, g + 1) for g in range(groups - 1)]
    earlier = lax.ppermute(coarse[3:], GROUP, hops)
    before = jnp.concatenate([earlier, coarse[:3]], axis=0)
    first = (jnp.arange(R) == 0)[None, :, None, None]
    field = blur_taps[:R][None, :, None, None] * coarse.astype(f32)[:, None]
    field = field + jnp.where(first, blur_taps[R] * before.astype(f32)[:, None], 0.0)
    field = field.astype(bf16).reshape(Y, C, X)
    g_out = lax.all_to_all(field, PLANE, 0, 0, tiled=True)

    taps = weight.reshape(3, 3, C, C)
    forward_mix = taps.transpose(0, 2, 1, 3).reshape(3 * C, 3 * C)
    backward_mix = taps.transpose(0, 3, 1, 2).reshape(3 * C, 3 * C)
    act = activations[:, 0].transpose(1, 0, 2)
    flops = 2 * Y * X * 9 * C * C
    slope, turned = call(
        forward_kernel,
        (shape((Y, C, X), f32), shape((Y * X, WIDE), bf16)),
        [pltpu.VMEM((3 * C, Y * X), bf16), pltpu.VMEM((C, (Y + 2) * X), f32)],
        flops,
        4 << 20,
        act,
        forward_mix,
        conv_bias[:, None],
    )
    grad, sums = call(
        weight_kernel,
        (shape((Y, C, X), bf16), shape((N_FLAT, PIECE, WIDE), f32)),
        [pltpu.VMEM((3 * C, Y * X), bf16)],
        flops,
        4 << 20,
        g_out,
        slope,
        turned,
    )
    out = call(
        input_kernel,
        shape((Y, C, X), bf16),
        [pltpu.VMEM((3 * C, Y * X), bf16), pltpu.VMEM((C, (Y + 2) * X), f32)],
        flops,
        2 << 20,
        grad,
        g_out,
        backward_mix,
    )
    grad_input = out.transpose(1, 0, 2)[:, None]

    parts = lax.all_to_all(sums, FLAT, 0, 0, tiled=True)
    sent = call(
        spread_sum_kernel, shape((N_COLUMN, PIECE, WIDE), f32), [], 1 << 16, 1 << 18, parts
    )
    parts = lax.all_to_all(sent, COLUMN, 0, 0, tiled=True)
    factor = float(512 * Y * X) ** -0.5
    sent = call(
        lambda a, b: scaled_sum_kernel(factor, a, b),
        shape((N_FLAT, PIECE, WIDE), f32),
        [],
        1 << 16,
        1 << 18,
        parts,
    )
    whole = lax.all_to_all(sent, FLAT, 0, 0, tiled=True).reshape(N_FLAT * PIECE, WIDE)
    grad_w = whole[: 3 * C, : 3 * C].reshape(3, C, 3, C).transpose(0, 2, 1, 3)
    return grad_input, grad_w.reshape(9, C, C), whole[3 * C, :C]


def solution(mesh):
    fine = Mesh(mesh.devices.reshape(SIZES), AXES)
    in_specs = (P(None, AXES, None, None), P(None, GROUP, PLANE, None), P(), P(), P())
    out_specs = (P(None, AXES, None, None), P(), P())
    return jax.shard_map(
        on_device, mesh=fine, in_specs=in_specs, out_specs=out_specs, check_vma=False
    )
```

```python
import jax
import jax.numpy as jnp
from jax import lax
from jax.experimental import pallas as pl
from jax.experimental.pallas import tpu as pltpu
from jax.sharding import Mesh
from jax.sharding import PartitionSpec as P

R = 8
C = 64
Y = 32
X = 128
AXES = ("zl", "core", "x", "y", "zh")
SIZES = (8, 2, 4, 4, 2)
GROUP = ("zl", "core")
PLANE = ("x", "y", "zh")
CROSS = ("x", "y")
N_CROSS = 16
FLAT = ("core", "x", "y")
COLUMN = ("zl", "zh")
N_FLAT = 32
N_GROUP = 16
N_COLUMN = 16
PIECE = 8
WIDE = 256
VMEM_LIMIT = 48 * 1024 * 1024


def shifted(row, step):
    if step == 0:
        return row
    lane = lax.broadcasted_iota(jnp.int32, row.shape, 1)
    edge = 0 if step < 0 else X - 1
    return jnp.where(lane == edge, 0.0, pltpu.roll(row, (-step) % X, 1))


def forward_kernel(act_ref, mix_ref, bias_ref, slope_ref, turned_ref, stack, hidden):
    column = lax.broadcasted_iota(jnp.int32, (X, WIDE - 3 * C), 1)
    ones = jnp.where(column == 0, 1.0, 0.0).astype(jnp.bfloat16)

    def spread(y, carry):
        row = act_ref[y].astype(jnp.float32)
        at = pl.ds(pl.multiple_of(y * X, X), X)
        whole = jnp.concatenate([shifted(row, b - 1) for b in range(3)], axis=0)
        stack[:, at] = whole.astype(jnp.bfloat16)
        turned_ref[at, : 3 * C] = whole.T.astype(jnp.bfloat16)
        turned_ref[at, 3 * C :] = ones
        return carry

    lax.fori_loop(0, Y, spread, 0)
    hidden[...] = jnp.broadcast_to(bias_ref[...], hidden.shape)

    def taps(j, carry):
        at = pl.multiple_of(j * 2 * X, 2 * X)
        part = jnp.dot(
            mix_ref[...], stack[:, pl.ds(at, 2 * X)], preferred_element_type=jnp.float32
        )
        for a in range(3):
            place = pl.ds(pl.multiple_of(at + (2 - a) * X, X), 2 * X)
            hidden[:, place] += part[a * C : (a + 1) * C]
        return carry

    lax.fori_loop(0, Y // 2, taps, 0)

    def slopes(y, carry):
        h = hidden[:, pl.ds(pl.multiple_of((y + 1) * X, X), X)]
        s = jax.nn.sigmoid(h)
        slope_ref[y] = s * (1.0 + h * (1.0 - s))
        return carry

    lax.fori_loop(0, Y, slopes, 0)


def weight_kernel(g_ref, slope_ref, turned_ref, grad_ref, sums_ref, stack):
    zero = jnp.zeros((C, X), jnp.bfloat16)
    stack[0:C, (Y - 1) * X :] = zero
    stack[2 * C :, 0:X] = zero
    for y in range(Y):
        grad = (g_ref[y].astype(jnp.float32) * slope_ref[y]).astype(jnp.bfloat16)
        grad_ref[y] = grad
        for a in range(3):
            row = y + a - 1
            if 0 <= row < Y:
                stack[a * C : (a + 1) * C, row * X : (row + 1) * X] = grad
    total = jnp.zeros((3 * C, WIDE), jnp.float32)
    for j in range(Y // 2):
        at = slice(j * 2 * X, (j + 1) * 2 * X)
        total += jnp.dot(stack[:, at], turned_ref[at, :], preferred_element_type=jnp.float32)
    sums_ref[: 3 * C // PIECE] = total.reshape(3 * C // PIECE, PIECE, WIDE)
    bias = total[C : 2 * C, 3 * C : 3 * C + 1]
    diagonal = lax.broadcasted_iota(jnp.int32, (C, WIDE), 0) == lax.broadcasted_iota(
        jnp.int32, (C, WIDE), 1
    )
    row = jnp.sum(jnp.where(diagonal, bias, 0.0), axis=0, keepdims=True)
    first = lax.broadcasted_iota(jnp.int32, (PIECE, WIDE), 0) == 0
    sums_ref[3 * C // PIECE] = jnp.where(first, row, 0.0)
    sums_ref[3 * C // PIECE + 1 :] = jnp.zeros(
        (N_FLAT - 3 * C // PIECE - 1, PIECE, WIDE), jnp.float32
    )


def input_kernel(grad_ref, g_ref, mix_ref, out_ref, stack, total):
    total[...] = jnp.zeros_like(total)

    def spread(y, carry):
        row = grad_ref[y].astype(jnp.float32)
        at = pl.ds(pl.multiple_of(y * X, X), X)
        whole = jnp.concatenate([shifted(row, 1 - b) for b in range(3)], axis=0)
        stack[:, at] = whole.astype(jnp.bfloat16)
        return carry

    lax.fori_loop(0, Y, spread, 0)

    def taps(j, carry):
        at = pl.multiple_of(j * 2 * X, 2 * X)
        part = jnp.dot(
            mix_ref[...], stack[:, pl.ds(at, 2 * X)], preferred_element_type=jnp.float32
        )
        for a in range(3):
            place = pl.ds(pl.multiple_of(at + a * X, X), 2 * X)
            total[:, place] += part[a * C : (a + 1) * C]
        return carry

    lax.fori_loop(0, Y // 2, taps, 0)

    def finish(y, carry):
        conv = total[:, pl.ds(pl.multiple_of((y + 1) * X, X), X)]
        out_ref[y] = (g_ref[y].astype(jnp.float32) + conv).astype(jnp.bfloat16)
        return carry

    lax.fori_loop(0, Y, finish, 0)


def blur_kernel(half_ref, taps_ref, own_ref, other_ref, halo_own_ref, halo_other_ref, out_ref):
    half = half_ref[0]
    spill = jnp.where(half == 0, taps_ref[R], 0.0)
    sides = ((half, own_ref, halo_own_ref), (1 - half, other_ref, halo_other_ref))
    for slot, rows_ref, halo_ref in sides:
        before = halo_ref[0].astype(jnp.float32)
        for k in range(4):
            row = rows_ref[k].astype(jnp.float32)
            for pair in range(4):
                value = taps_ref[2 * pair + half] * row
                if pair == 0:
                    value = value + spill * before
                out_ref[4 * k + pair, slot] = value.astype(jnp.bfloat16)
            before = row


def unpack_kernel(whole_ref, weight_ref, bias_ref):
    for a in range(3):
        rows = whole_ref[a * C : (a + 1) * C]
        for b in range(3):
            weight_ref[3 * a + b] = rows[:, b * C : (b + 1) * C]
    bias_ref[...] = whole_ref[3 * C : 3 * C + 1, :C]


def spread_sum_kernel(parts_ref, out_ref):
    total = jnp.sum(parts_ref[...], axis=0)
    for copy in range(out_ref.shape[0]):
        out_ref[copy] = total


def scaled_sum_kernel(factor, parts_ref, out_ref):
    total = jnp.sum(parts_ref[...], axis=0) * factor
    for copy in range(out_ref.shape[0]):
        out_ref[copy] = total


def call(kernel, outs, scratch, flops, moved, *args, scalars=0):
    return pl.pallas_call(
        kernel,
        out_shape=outs,
        in_specs=[pl.BlockSpec(memory_space=pltpu.SMEM)] * scalars
        + [pl.BlockSpec(memory_space=pltpu.VMEM)] * (len(args) - scalars),
        out_specs=jax.tree.map(lambda _: pl.BlockSpec(memory_space=pltpu.VMEM), outs),
        scratch_shapes=scratch,
        compiler_params=pltpu.CompilerParams(vmem_limit_bytes=VMEM_LIMIT),
        cost_estimate=pl.CostEstimate(flops=flops, bytes_accessed=moved, transcendentals=0),
    )(*args)


def on_device(activations, cotangent, weight, conv_bias, blur_taps):
    shape = jax.ShapeDtypeStruct
    bf16, f32 = jnp.bfloat16, jnp.float32
    coarse = cotangent[:, :, 0, :].transpose(1, 0, 2)
    other = lax.ppermute(coarse, "zh", [(0, 1), (1, 0)])
    halos = []
    for side in range(2):
        pairs = []
        for group in range(N_GROUP - 1):
            for cross in range(N_CROSS):
                source = (group * N_CROSS + cross) * 2 + side
                pairs.append((source, ((group + 1) * N_CROSS + cross) * 2))
        halos.append(lax.ppermute(coarse[3:], AXES, pairs))
    half = lax.axis_index("zh").astype(jnp.int32)
    field = call(
        blur_kernel,
        shape((N_CROSS, 2, C, X), bf16),
        [],
        1 << 20,
        1 << 20,
        half[None],
        blur_taps,
        coarse,
        other,
        *halos,
        scalars=2,
    )
    g_out = lax.all_to_all(field, CROSS, 0, 0, tiled=True).reshape(Y, C, X)

    taps = weight.reshape(3, 3, C, C)
    forward_mix = taps.transpose(0, 2, 1, 3).reshape(3 * C, 3 * C)
    backward_mix = taps.transpose(0, 3, 1, 2).reshape(3 * C, 3 * C)
    act = activations[:, 0].transpose(1, 0, 2)
    flops = 2 * Y * X * 9 * C * C
    slope, turned = call(
        forward_kernel,
        (shape((Y, C, X), f32), shape((Y * X, WIDE), bf16)),
        [pltpu.VMEM((3 * C, Y * X), bf16), pltpu.VMEM((C, (Y + 2) * X), f32)],
        flops,
        4 << 20,
        act,
        forward_mix,
        conv_bias[:, None],
    )
    grad, sums = call(
        weight_kernel,
        (shape((Y, C, X), bf16), shape((N_FLAT, PIECE, WIDE), f32)),
        [pltpu.VMEM((3 * C, Y * X), bf16)],
        flops,
        4 << 20,
        g_out,
        slope,
        turned,
    )
    out = call(
        input_kernel,
        shape((Y, C, X), bf16),
        [pltpu.VMEM((3 * C, Y * X), bf16), pltpu.VMEM((C, (Y + 2) * X), f32)],
        flops,
        2 << 20,
        grad,
        g_out,
        backward_mix,
    )
    grad_input = out.transpose(1, 0, 2)[:, None]

    parts = lax.all_to_all(sums, FLAT, 0, 0, tiled=True)
    sent = call(
        spread_sum_kernel, shape((N_COLUMN, PIECE, WIDE), f32), [], 1 << 16, 1 << 18, parts
    )
    parts = lax.all_to_all(sent, COLUMN, 0, 0, tiled=True)
    parts, grad_input = lax.optimization_barrier((parts, grad_input))
    factor = float(512 * Y * X) ** -0.5
    sent = call(
        lambda a, b: scaled_sum_kernel(factor, a, b),
        shape((N_FLAT, PIECE, WIDE), f32),
        [],
        1 << 16,
        1 << 18,
        parts,
    )
    whole = lax.all_to_all(sent, FLAT, 0, 0, tiled=True).reshape(N_FLAT * PIECE, WIDE)
    grad_w, grad_b = call(
        unpack_kernel, (shape((9, C, C), f32), shape((1, C), f32)), [], 1, 1 << 18, whole
    )
    return grad_input, grad_w, grad_b.reshape(C)


def solution(mesh):
    fine = Mesh(mesh.devices.reshape(SIZES), AXES)
    in_specs = (P(None, AXES, None, None), P(None, GROUP, PLANE, None), P(), P(), P())
    out_specs = (P(None, AXES, None, None), P(), P())
    return jax.shard_map(
        on_device, mesh=fine, in_specs=in_specs, out_specs=out_specs, check_vma=False
    )
```

```python
import jax
import jax.numpy as jnp
from jax import lax
from jax.experimental import pallas as pl
from jax.experimental.pallas import tpu as pltpu
from jax.sharding import Mesh
from jax.sharding import PartitionSpec as P

R = 8
C = 64
Y = 32
X = 128
AXES = ("zl", "core", "x", "y", "zh")
SIZES = (8, 2, 4, 4, 2)
GROUP = ("zl", "core")
PLANE = ("x", "y", "zh")
CROSS = ("x", "y")
N_CROSS = 16
FLAT = ("core", "x", "y")
COLUMN = ("zl", "zh")
N_FLAT = 32
N_GROUP = 16
N_COLUMN = 16
PIECE = 8
WIDE = 256
VMEM_LIMIT = 16 * 1024 * 1024


def shifted(row, step):
    if step == 0:
        return row
    lane = lax.broadcasted_iota(jnp.int32, row.shape, 1)
    edge = 0 if step < 0 else X - 1
    return jnp.where(lane == edge, 0.0, pltpu.roll(row, (-step) % X, 1))


def forward_kernel(
    half_ref,
    taps_ref,
    bias_ref,
    act_far,
    weight_far,
    slope_ref,
    turned_ref,
    coef_ref,
    stack,
    hidden,
    act_ref,
    weight_ref,
    sems,
):
    copies = [
        pltpu.make_async_copy(act_far, act_ref, sems.at[0]),
        pltpu.make_async_copy(weight_far, weight_ref, sems.at[1]),
    ]
    for copy in copies:
        copy.start()
    half = half_ref[0]
    for pair in range(4):
        coef_ref[pair : pair + 1] = jnp.full((1, X), taps_ref[2 * pair + half], jnp.float32)
    spill = jnp.where(half == 0, taps_ref[R], 0.0)
    coef_ref[4:] = jnp.full((4, X), spill, jnp.float32)
    column = lax.broadcasted_iota(jnp.int32, (X, WIDE - 3 * C), 1)
    ones = jnp.where(column == 0, 1.0, 0.0).astype(jnp.bfloat16)
    for copy in copies:
        copy.wait()
    for y in range(Y):
        if y % 16 == 0:
            rows = jnp.swapaxes(act_ref[:, y : y + 16].astype(jnp.float32), 0, 1)
        row = rows[y % 16]
        at = slice(y * X, (y + 1) * X)
        whole = jnp.concatenate([shifted(row, b - 1) for b in range(3)], axis=0)
        stack[:, at] = whole.astype(jnp.bfloat16)
        turned_ref[at, : 3 * C] = whole.T.astype(jnp.bfloat16)
        turned_ref[at, 3 * C :] = ones
    square = (C, C)
    diagonal = lax.broadcasted_iota(jnp.int32, square, 0) == lax.broadcasted_iota(
        jnp.int32, square, 1
    )
    bias = jnp.sum(jnp.where(diagonal, bias_ref[...], 0.0), axis=1, keepdims=True)
    hidden[...] = jnp.broadcast_to(bias, hidden.shape)
    mix = jnp.concatenate(
        [jnp.concatenate([weight_ref[3 * a + b] for b in range(3)], axis=1) for a in range(3)],
        axis=0,
    )
    for j in range(Y // 2):
        at = j * 2 * X
        part = jnp.dot(mix, stack[:, at : at + 2 * X], preferred_element_type=jnp.float32)
        for a in range(3):
            place = slice(at + (2 - a) * X, at + (4 - a) * X)
            hidden[:, place] += part[a * C : (a + 1) * C]
    for y in range(Y):
        h = hidden[:, (y + 1) * X : (y + 2) * X]
        s = jax.nn.sigmoid(h)
        slope_ref[y] = s * (1.0 + h * (1.0 - s))


def weight_kernel(g_ref, slope_ref, turned_ref, grad_ref, sums_ref, stack):
    zero = jnp.zeros((C, X), jnp.bfloat16)
    stack[0:C, (Y - 1) * X :] = zero
    stack[2 * C :, 0:X] = zero
    for y in range(Y):
        grad = (g_ref[y].astype(jnp.float32) * slope_ref[y]).astype(jnp.bfloat16)
        grad_ref[y] = grad
        for a in range(3):
            row = y + a - 1
            if 0 <= row < Y:
                stack[a * C : (a + 1) * C, row * X : (row + 1) * X] = grad
    total = jnp.zeros((3 * C, WIDE), jnp.float32)
    for j in range(Y // 2):
        at = slice(j * 2 * X, (j + 1) * 2 * X)
        total += jnp.dot(stack[:, at], turned_ref[at, :], preferred_element_type=jnp.float32)
    sums_ref[: 3 * C // PIECE] = total.reshape(3 * C // PIECE, PIECE, WIDE)
    bias = total[C : 2 * C, 3 * C : 3 * C + 1]
    diagonal = lax.broadcasted_iota(jnp.int32, (C, WIDE), 0) == lax.broadcasted_iota(
        jnp.int32, (C, WIDE), 1
    )
    row = jnp.sum(jnp.where(diagonal, bias, 0.0), axis=0, keepdims=True)
    first = lax.broadcasted_iota(jnp.int32, (PIECE, WIDE), 0) == 0
    sums_ref[3 * C // PIECE] = jnp.where(first, row, 0.0)
    sums_ref[3 * C // PIECE + 1 :] = jnp.zeros(
        (N_FLAT - 3 * C // PIECE - 1, PIECE, WIDE), jnp.float32
    )


def input_kernel(grad_ref, g_ref, weight_ref, out_ref, stack, total):
    total[...] = jnp.zeros_like(total)
    for y in range(Y):
        row = grad_ref[y].astype(jnp.float32)
        whole = jnp.concatenate([shifted(row, 1 - b) for b in range(3)], axis=0)
        stack[:, y * X : (y + 1) * X] = whole.astype(jnp.bfloat16)
    mix = jnp.concatenate(
        [
            jnp.concatenate(
                [weight_ref[3 * a + b].astype(jnp.float32).T for b in range(3)], axis=1
            )
            for a in range(3)
        ],
        axis=0,
    ).astype(jnp.bfloat16)
    for j in range(Y // 2):
        at = j * 2 * X
        part = jnp.dot(mix, stack[:, at : at + 2 * X], preferred_element_type=jnp.float32)
        for a in range(3):
            place = slice(at + a * X, at + (a + 2) * X)
            total[:, place] += part[a * C : (a + 1) * C]
    for y in range(Y):
        conv = total[:, (y + 1) * X : (y + 2) * X]
        out_ref[y] = (g_ref[y].astype(jnp.float32) + conv).astype(jnp.bfloat16)


def blur_kernel(half_ref, taps_ref, own_ref, other_ref, halo_own_ref, halo_other_ref, out_ref):
    half = half_ref[0]
    sides = ((half, own_ref, halo_own_ref), (1 - half, other_ref, halo_other_ref))
    for slot, rows_ref, halo_ref in sides:
        before = halo_ref[0].astype(jnp.float32)
        for k in range(4):
            row = rows_ref[k].astype(jnp.float32)
            for pair in range(4):
                value = taps_ref[pair : pair + 1] * row
                if pair == 0:
                    value = value + taps_ref[4:5] * before
                out_ref[4 * k + pair, slot] = value.astype(jnp.bfloat16)
            before = row


def unpack_kernel(whole_ref, weight_ref, bias_ref):
    for a in range(3):
        rows = whole_ref[a * C : (a + 1) * C]
        for b in range(3):
            weight_ref[3 * a + b] = rows[:, b * C : (b + 1) * C]
    bias_ref[...] = whole_ref[3 * C : 3 * C + 1, :C]


def spread_sum_kernel(parts_ref, out_ref):
    total = jnp.sum(parts_ref[...], axis=0)
    for copy in range(out_ref.shape[0]):
        out_ref[copy] = total


def scaled_sum_kernel(factor, parts_ref, out_ref):
    total = jnp.sum(parts_ref[...], axis=0) * factor
    for copy in range(out_ref.shape[0]):
        out_ref[copy] = total


def call(kernel, outs, scratch, flops, moved, *args, scalars=0, far=0):
    return pl.pallas_call(
        kernel,
        out_shape=outs,
        in_specs=[pl.BlockSpec(memory_space=pltpu.SMEM)] * scalars
        + [pl.BlockSpec(memory_space=pltpu.VMEM)] * (len(args) - scalars - far)
        + [pl.BlockSpec(memory_space=pltpu.HBM)] * far,
        out_specs=jax.tree.map(lambda _: pl.BlockSpec(memory_space=pltpu.VMEM), outs),
        scratch_shapes=scratch,
        compiler_params=pltpu.CompilerParams(vmem_limit_bytes=VMEM_LIMIT),
        cost_estimate=pl.CostEstimate(flops=flops, bytes_accessed=moved, transcendentals=0),
    )(*args)


def on_device(activations, cotangent, weight, conv_bias, blur_taps):
    shape = jax.ShapeDtypeStruct
    bf16, f32 = jnp.bfloat16, jnp.float32
    coarse = cotangent[:, :, 0, :].transpose(1, 0, 2)
    hops = [
        [
            ((group * N_CROSS + cross) * 2 + side, ((group + 1) * N_CROSS + cross) * 2)
            for group in range(N_GROUP - 1)
            for cross in range(N_CROSS)
        ]
        for side in range(2)
    ]
    halo_other = lax.ppermute(coarse[3:], AXES, hops[1])
    other = lax.ppermute(coarse, "zh", [(0, 1), (1, 0)])
    halo_own = lax.ppermute(coarse[3:], AXES, hops[0])
    half = lax.axis_index("zh").astype(jnp.int32)[None]
    flops = 2 * Y * X * 9 * C * C
    slope, turned, coef = call(
        forward_kernel,
        (shape((Y, C, X), f32), shape((Y * X, WIDE), bf16), shape((8, X), f32)),
        [
            pltpu.VMEM((3 * C, Y * X), bf16),
            pltpu.VMEM((C, (Y + 2) * X), f32),
            pltpu.VMEM((C, Y, X), bf16),
            pltpu.VMEM((9, C, C), bf16),
            pltpu.SemaphoreType.DMA((2,)),
        ],
        64 * flops,
        128 << 20,
        half,
        blur_taps,
        conv_bias[None, :],
        activations[:, 0],
        weight,
        scalars=2,
        far=2,
    )
    slope, turned, coef, halo_other, halo_own, other = lax.optimization_barrier(
        (slope, turned, coef, halo_other, halo_own, other)
    )
    field = call(
        blur_kernel,
        shape((N_CROSS, 2, C, X), bf16),
        [],
        1 << 20,
        1 << 20,
        half,
        coef,
        coarse,
        other,
        halo_own,
        halo_other,
        scalars=1,
    )
    g_out = lax.all_to_all(field, CROSS, 0, 0, tiled=True).reshape(Y, C, X)
    grad, sums = call(
        weight_kernel,
        (shape((Y, C, X), bf16), shape((N_FLAT, PIECE, WIDE), f32)),
        [pltpu.VMEM((3 * C, Y * X), bf16)],
        flops,
        4 << 20,
        g_out,
        slope,
        turned,
    )
    out = call(
        input_kernel,
        shape((Y, C, X), bf16),
        [pltpu.VMEM((3 * C, Y * X), bf16), pltpu.VMEM((C, (Y + 2) * X), f32)],
        flops,
        2 << 20,
        grad,
        g_out,
        weight,
    )
    grad_input = out.transpose(1, 0, 2)[:, None]

    parts = lax.all_to_all(sums, FLAT, 0, 0, tiled=True)
    sent = call(
        spread_sum_kernel, shape((N_COLUMN, PIECE, WIDE), f32), [], 1 << 16, 1 << 18, parts
    )
    parts = lax.all_to_all(sent, COLUMN, 0, 0, tiled=True)
    parts, grad_input = lax.optimization_barrier((parts, grad_input))
    factor = float(512 * Y * X) ** -0.5
    sent = call(
        lambda a, b: scaled_sum_kernel(factor, a, b),
        shape((N_FLAT, PIECE, WIDE), f32),
        [],
        1 << 16,
        1 << 18,
        parts,
    )
    whole = lax.all_to_all(sent, FLAT, 0, 0, tiled=True).reshape(N_FLAT * PIECE, WIDE)
    grad_w, grad_b = call(
        unpack_kernel, (shape((9, C, C), f32), shape((1, C), f32)), [], 1, 1 << 18, whole
    )
    return grad_input, grad_w, grad_b.reshape(C)


def solution(mesh):
    fine = Mesh(mesh.devices.reshape(SIZES), AXES)
    in_specs = (P(None, AXES, None, None), P(None, GROUP, PLANE, None), P(), P(), P())
    out_specs = (P(None, AXES, None, None), P(), P())
    return jax.shard_map(
        on_device, mesh=fine, in_specs=in_specs, out_specs=out_specs, check_vma=False
    )
```

```python
import jax
import jax.numpy as jnp
from jax import lax
from jax.experimental import pallas as pl
from jax.experimental.pallas import tpu as pltpu
from jax.sharding import Mesh
from jax.sharding import PartitionSpec as P

R = 8
C = 64
Y = 32
X = 128
AXES = ("zl", "core", "x", "y", "zh")
SIZES = (8, 2, 4, 4, 2)
GROUP = ("zl", "core")
PLANE = ("x", "y", "zh")
CROSS = ("x", "y")
N_CROSS = 16
FLAT = ("core", "x", "y")
COLUMN = ("zl", "zh")
N_FLAT = 32
N_GROUP = 16
N_COLUMN = 16
PIECE = 4
LONG = 384
WIDE = 256
VMEM_LIMIT = 16 * 1024 * 1024


def shifted(row, step):
    if step == 0:
        return row
    lane = lax.broadcasted_iota(jnp.int32, row.shape, 1)
    edge = 0 if step < 0 else X - 1
    return jnp.where(lane == edge, 0.0, pltpu.roll(row, (-step) % X, 1))


def forward_kernel(
    half_ref,
    taps_ref,
    bias_ref,
    act_far,
    weight_far,
    slope_ref,
    turned_ref,
    coef_ref,
    stack,
    hidden,
    act_ref,
    weight_ref,
    sems,
):
    copies = [
        pltpu.make_async_copy(act_far, act_ref, sems.at[0]),
        pltpu.make_async_copy(weight_far, weight_ref, sems.at[1]),
    ]
    for copy in copies:
        copy.start()
    half = half_ref[0]
    for pair in range(4):
        coef_ref[pair : pair + 1] = jnp.full((1, X), taps_ref[2 * pair + half], jnp.float32)
    spill = jnp.where(half == 0, taps_ref[R], 0.0)
    coef_ref[4:] = jnp.full((4, X), spill, jnp.float32)
    column = lax.broadcasted_iota(jnp.int32, (X, WIDE - 3 * C), 1)
    ones = jnp.where(column == 0, 1.0, 0.0).astype(jnp.bfloat16)
    for copy in copies:
        copy.wait()
    for y in range(Y):
        if y % 16 == 0:
            rows = jnp.swapaxes(act_ref[:, y : y + 16].astype(jnp.float32), 0, 1)
        row = rows[y % 16]
        at = slice(y * X, (y + 1) * X)
        whole = jnp.concatenate([shifted(row, b - 1) for b in range(3)], axis=0)
        stack[:, at] = whole.astype(jnp.bfloat16)
        turned_ref[at, : 3 * C] = whole.T.astype(jnp.bfloat16)
        turned_ref[at, 3 * C :] = ones
    square = (C, C)
    diagonal = lax.broadcasted_iota(jnp.int32, square, 0) == lax.broadcasted_iota(
        jnp.int32, square, 1
    )
    bias = jnp.sum(jnp.where(diagonal, bias_ref[...], 0.0), axis=1, keepdims=True)
    hidden[...] = jnp.broadcast_to(bias, hidden.shape)
    mix = jnp.concatenate(
        [jnp.concatenate([weight_ref[3 * a + b] for b in range(3)], axis=1) for a in range(3)],
        axis=0,
    )
    for j in range(Y // 2):
        at = j * 2 * X
        part = jnp.dot(mix, stack[:, at : at + 2 * X], preferred_element_type=jnp.float32)
        for a in range(3):
            place = slice(at + (2 - a) * X, at + (4 - a) * X)
            hidden[:, place] += part[a * C : (a + 1) * C]
    for y in range(Y):
        h = hidden[:, (y + 1) * X : (y + 2) * X]
        s = jax.nn.sigmoid(h)
        slope_ref[y] = s * (1.0 + h * (1.0 - s))


def weight_kernel(g_ref, slope_ref, turned_ref, grad_ref, sums_ref, stack):
    zero = jnp.zeros((C, X), jnp.bfloat16)
    stack[0:C, (Y - 1) * X :] = zero
    stack[2 * C :, 0:X] = zero
    for y in range(Y):
        grad = (g_ref[y].astype(jnp.float32) * slope_ref[y]).astype(jnp.bfloat16)
        grad_ref[y] = grad
        for a in range(3):
            row = y + a - 1
            if 0 <= row < Y:
                stack[a * C : (a + 1) * C, row * X : (row + 1) * X] = grad
    total = jnp.zeros((3 * C, WIDE), jnp.float32)
    for j in range(Y // 2):
        at = slice(j * 2 * X, (j + 1) * 2 * X)
        total += jnp.dot(stack[:, at], turned_ref[at, :], preferred_element_type=jnp.float32)
    square = (C, C)
    diagonal = lax.broadcasted_iota(jnp.int32, square, 0) == lax.broadcasted_iota(
        jnp.int32, square, 1
    )
    bias = total[C : 2 * C, 3 * C : 3 * C + 1]
    row = jnp.sum(jnp.where(diagonal, bias, 0.0), axis=0, keepdims=True)
    first = lax.broadcasted_iota(jnp.int32, square, 0) == 0
    zero = jnp.zeros(square, jnp.float32)
    sides = [total[a * C : (a + 1) * C, 2 * C : 3 * C] for a in range(3)]
    low = jnp.concatenate([sides[0], sides[1]], axis=1)
    high = jnp.concatenate([sides[2], zero], axis=1)
    last = jnp.concatenate([jnp.where(first, row, 0.0), zero], axis=1)
    top = jnp.concatenate([total[:C, : 2 * C], total[2 * C :, : 2 * C], high], axis=1)
    bottom = jnp.concatenate([total[C : 2 * C, : 2 * C], low, last], axis=1)
    for half, block in enumerate((top, bottom)):
        for piece in range(C // PIECE):
            sums_ref[half * C // PIECE + piece] = block[piece * PIECE : (piece + 1) * PIECE]


def input_kernel(grad_ref, g_ref, weight_ref, out_ref, stack, total):
    total[...] = jnp.zeros_like(total)
    for y in range(Y):
        row = grad_ref[y].astype(jnp.float32)
        whole = jnp.concatenate([shifted(row, 1 - b) for b in range(3)], axis=0)
        stack[:, y * X : (y + 1) * X] = whole.astype(jnp.bfloat16)
    mix = jnp.concatenate(
        [
            jnp.concatenate(
                [weight_ref[3 * a + b].astype(jnp.float32).T for b in range(3)], axis=1
            )
            for a in range(3)
        ],
        axis=0,
    ).astype(jnp.bfloat16)
    for j in range(Y // 2):
        at = j * 2 * X
        part = jnp.dot(mix, stack[:, at : at + 2 * X], preferred_element_type=jnp.float32)
        for a in range(3):
            place = slice(at + a * X, at + (a + 2) * X)
            total[:, place] += part[a * C : (a + 1) * C]
    for y in range(Y):
        conv = total[:, (y + 1) * X : (y + 2) * X]
        out_ref[y] = (g_ref[y].astype(jnp.float32) + conv).astype(jnp.bfloat16)


def blur_kernel(half_ref, taps_ref, own_ref, other_ref, halo_own_ref, halo_other_ref, out_ref):
    half = half_ref[0]
    sides = ((half, own_ref, halo_own_ref), (1 - half, other_ref, halo_other_ref))
    for slot, rows_ref, halo_ref in sides:
        before = halo_ref[0].astype(jnp.float32)
        for k in range(4):
            row = rows_ref[k].astype(jnp.float32)
            for pair in range(4):
                value = taps_ref[pair : pair + 1] * row
                if pair == 0:
                    value = value + taps_ref[4:5] * before
                out_ref[4 * k + pair, slot] = value.astype(jnp.bfloat16)
            before = row


def unpack_kernel(whole_ref, weight_ref, bias_ref):
    top, bottom = (
        jnp.concatenate(
            [whole_ref[half * C // PIECE + piece] for piece in range(C // PIECE)], axis=0
        )
        for half in range(2)
    )
    rows = (
        (top, 0),
        (top, 1),
        (bottom, 2),
        (bottom, 0),
        (bottom, 1),
        (bottom, 3),
        (top, 2),
        (top, 3),
        (top, 4),
    )
    for tap, (block, place) in enumerate(rows):
        weight_ref[tap] = block[:, place * C : (place + 1) * C]
    bias_ref[...] = bottom[0:1, 4 * C : 5 * C]


def spread_sum_kernel(parts_ref, out_ref):
    total = jnp.sum(parts_ref[...], axis=0)
    for copy in range(out_ref.shape[0]):
        out_ref[copy] = total


def scaled_sum_kernel(factor, parts_ref, out_ref):
    total = jnp.sum(parts_ref[...], axis=0) * factor
    for copy in range(out_ref.shape[0]):
        out_ref[copy] = total


def call(kernel, outs, scratch, flops, moved, *args, scalars=0, far=0):
    return pl.pallas_call(
        kernel,
        out_shape=outs,
        in_specs=[pl.BlockSpec(memory_space=pltpu.SMEM)] * scalars
        + [pl.BlockSpec(memory_space=pltpu.VMEM)] * (len(args) - scalars - far)
        + [pl.BlockSpec(memory_space=pltpu.HBM)] * far,
        out_specs=jax.tree.map(lambda _: pl.BlockSpec(memory_space=pltpu.VMEM), outs),
        scratch_shapes=scratch,
        compiler_params=pltpu.CompilerParams(vmem_limit_bytes=VMEM_LIMIT),
        cost_estimate=pl.CostEstimate(flops=flops, bytes_accessed=moved, transcendentals=0),
    )(*args)


def on_device(activations, cotangent, weight, conv_bias, blur_taps):
    shape = jax.ShapeDtypeStruct
    bf16, f32 = jnp.bfloat16, jnp.float32
    coarse = cotangent[:, :, 0, :].transpose(1, 0, 2)
    hops = [
        [
            ((group * N_CROSS + cross) * 2 + side, ((group + 1) * N_CROSS + cross) * 2)
            for group in range(N_GROUP - 1)
            for cross in range(N_CROSS)
        ]
        for side in range(2)
    ]
    halo_other = lax.ppermute(coarse[3:], AXES, hops[1])
    other = lax.ppermute(coarse, "zh", [(0, 1), (1, 0)])
    halo_own = lax.ppermute(coarse[3:], AXES, hops[0])
    half = lax.axis_index("zh").astype(jnp.int32)[None]
    flops = 2 * Y * X * 9 * C * C
    slope, turned, coef = call(
        forward_kernel,
        (shape((Y, C, X), f32), shape((Y * X, WIDE), bf16), shape((8, X), f32)),
        [
            pltpu.VMEM((3 * C, Y * X), bf16),
            pltpu.VMEM((C, (Y + 2) * X), f32),
            pltpu.VMEM((C, Y, X), bf16),
            pltpu.VMEM((9, C, C), bf16),
            pltpu.SemaphoreType.DMA((2,)),
        ],
        64 * flops,
        128 << 20,
        half,
        blur_taps,
        conv_bias[None, :],
        activations[:, 0],
        weight,
        scalars=2,
        far=2,
    )
    slope, turned, coef, halo_own, halo_other, other = lax.optimization_barrier(
        (slope, turned, coef, halo_own, halo_other, other)
    )
    field = call(
        blur_kernel,
        shape((N_CROSS, 2, C, X), bf16),
        [],
        1 << 20,
        1 << 20,
        half,
        coef,
        coarse,
        other,
        halo_own,
        halo_other,
        scalars=1,
    )
    g_out = lax.all_to_all(field, CROSS, 0, 0, tiled=True).reshape(Y, C, X)
    grad, sums = call(
        weight_kernel,
        (shape((Y, C, X), bf16), shape((N_FLAT, PIECE, LONG), f32)),
        [pltpu.VMEM((3 * C, Y * X), bf16)],
        flops,
        4 << 20,
        g_out,
        slope,
        turned,
    )
    out = call(
        input_kernel,
        shape((Y, C, X), bf16),
        [pltpu.VMEM((3 * C, Y * X), bf16), pltpu.VMEM((C, (Y + 2) * X), f32)],
        flops,
        2 << 20,
        grad,
        g_out,
        weight,
    )
    grad_input = out.transpose(1, 0, 2)[:, None]

    parts = lax.all_to_all(sums, FLAT, 0, 0, tiled=True)
    sent = call(
        spread_sum_kernel, shape((N_COLUMN, PIECE, LONG), f32), [], 1 << 16, 1 << 18, parts
    )
    parts = lax.all_to_all(sent, COLUMN, 0, 0, tiled=True)
    parts, grad_input = lax.optimization_barrier((parts, grad_input))
    factor = float(512 * Y * X) ** -0.5
    sent = call(
        lambda a, b: scaled_sum_kernel(factor, a, b),
        shape((N_FLAT, PIECE, LONG), f32),
        [],
        1 << 16,
        1 << 18,
        parts,
    )
    whole = lax.all_to_all(sent, FLAT, 0, 0, tiled=True)
    grad_w, grad_b = call(
        unpack_kernel, (shape((9, C, C), f32), shape((1, C), f32)), [], 1, 1 << 18, whole
    )
    return grad_input, grad_w, grad_b.reshape(C)


def solution(mesh):
    fine = Mesh(mesh.devices.reshape(SIZES), AXES)
    in_specs = (P(None, AXES, None, None), P(None, GROUP, PLANE, None), P(), P(), P())
    out_specs = (P(None, AXES, None, None), P(), P())
    return jax.shard_map(
        on_device, mesh=fine, in_specs=in_specs, out_specs=out_specs, check_vma=False
    )
```

```python
import jax
import jax.numpy as jnp
from jax import lax
from jax.experimental import pallas as pl
from jax.experimental.pallas import tpu as pltpu
from jax.sharding import Mesh
from jax.sharding import PartitionSpec as P

R = 8
C = 64
Y = 32
X = 128
AXES = ("zl", "core", "x", "y", "zh")
SIZES = (8, 2, 4, 4, 2)
GROUP = ("zl", "core")
PLANE = ("x", "y", "zh")
CROSS = ("x", "y")
N_CROSS = 16
FLAT = ("core", "x", "y")
COLUMN = ("zl", "zh")
N_FLAT = 32
N_GROUP = 16
N_COLUMN = 16
FIRST = 6
PIECE = 4
LONG = 384
WIDE = 256
VMEM_LIMIT = 16 * 1024 * 1024


def shifted(row, step):
    if step == 0:
        return row
    lane = lax.broadcasted_iota(jnp.int32, row.shape, 1)
    edge = 0 if step < 0 else X - 1
    return jnp.where(lane == edge, 0.0, pltpu.roll(row, (-step) % X, 1))


def forward_kernel(
    half_ref,
    taps_ref,
    bias_ref,
    act_far,
    weight_far,
    slope_ref,
    turned_ref,
    coef_ref,
    stack,
    hidden,
    act_ref,
    weight_ref,
    sems,
):
    copies = [
        pltpu.make_async_copy(act_far, act_ref, sems.at[0]),
        pltpu.make_async_copy(weight_far, weight_ref, sems.at[1]),
    ]
    for copy in copies:
        copy.start()
    half = half_ref[0]
    for pair in range(4):
        coef_ref[pair : pair + 1] = jnp.full((1, X), taps_ref[2 * pair + half], jnp.float32)
    spill = jnp.where(half == 0, taps_ref[R], 0.0)
    coef_ref[4:] = jnp.full((4, X), spill, jnp.float32)
    column = lax.broadcasted_iota(jnp.int32, (X, WIDE - 3 * C), 1)
    ones = jnp.where(column == 0, 1.0, 0.0).astype(jnp.bfloat16)
    for copy in copies:
        copy.wait()
    for y in range(Y):
        if y % 16 == 0:
            rows = jnp.swapaxes(act_ref[:, y : y + 16].astype(jnp.float32), 0, 1)
        row = rows[y % 16]
        at = slice(y * X, (y + 1) * X)
        whole = jnp.concatenate([shifted(row, b - 1) for b in range(3)], axis=0)
        stack[:, at] = whole.astype(jnp.bfloat16)
        turned_ref[at, : 3 * C] = whole.T.astype(jnp.bfloat16)
        turned_ref[at, 3 * C :] = ones
    square = (C, C)
    diagonal = lax.broadcasted_iota(jnp.int32, square, 0) == lax.broadcasted_iota(
        jnp.int32, square, 1
    )
    bias = jnp.sum(jnp.where(diagonal, bias_ref[...], 0.0), axis=1, keepdims=True)
    hidden[...] = jnp.broadcast_to(bias, hidden.shape)
    mix = jnp.concatenate(
        [jnp.concatenate([weight_ref[3 * a + b] for b in range(3)], axis=1) for a in range(3)],
        axis=0,
    )
    for j in range(Y // 2):
        at = j * 2 * X
        part = jnp.dot(mix, stack[:, at : at + 2 * X], preferred_element_type=jnp.float32)
        for a in range(3):
            place = slice(at + (2 - a) * X, at + (4 - a) * X)
            hidden[:, place] += part[a * C : (a + 1) * C]
    for y in range(Y):
        h = hidden[:, (y + 1) * X : (y + 2) * X]
        s = jax.nn.sigmoid(h)
        slope_ref[y] = s * (1.0 + h * (1.0 - s))


def weight_kernel(g_ref, slope_ref, turned_ref, grad_ref, sums_ref, stack):
    zero = jnp.zeros((C, X), jnp.bfloat16)
    stack[0:C, (Y - 1) * X :] = zero
    stack[2 * C :, 0:X] = zero
    for y in range(Y):
        grad = (g_ref[y].astype(jnp.float32) * slope_ref[y]).astype(jnp.bfloat16)
        grad_ref[y] = grad
        for a in range(3):
            row = y + a - 1
            if 0 <= row < Y:
                stack[a * C : (a + 1) * C, row * X : (row + 1) * X] = grad
    total = jnp.zeros((3 * C, WIDE), jnp.float32)
    for j in range(Y // 2):
        at = slice(j * 2 * X, (j + 1) * 2 * X)
        total += jnp.dot(stack[:, at], turned_ref[at, :], preferred_element_type=jnp.float32)
    square = (C, C)
    diagonal = lax.broadcasted_iota(jnp.int32, square, 0) == lax.broadcasted_iota(
        jnp.int32, square, 1
    )
    bias = total[C : 2 * C, 3 * C : 3 * C + 1]
    row = jnp.sum(jnp.where(diagonal, bias, 0.0), axis=0, keepdims=True)
    first = lax.broadcasted_iota(jnp.int32, square, 0) == 0
    zero = jnp.zeros(square, jnp.float32)
    sides = [total[a * C : (a + 1) * C, 2 * C : 3 * C] for a in range(3)]
    low = jnp.concatenate([sides[0], sides[1]], axis=1)
    high = jnp.concatenate([sides[2], zero], axis=1)
    last = jnp.concatenate([jnp.where(first, row, 0.0), zero], axis=1)
    top = jnp.concatenate([total[:C, : 2 * C], total[2 * C :, : 2 * C], high], axis=1)
    bottom = jnp.concatenate([total[C : 2 * C, : 2 * C], low, last], axis=1)
    for half, block in enumerate((top, bottom)):
        for piece in range(C // PIECE):
            sums_ref[half * C // PIECE + piece] = block[piece * PIECE : (piece + 1) * PIECE]


def input_kernel(grad_ref, g_ref, weight_ref, out_ref, stack, total):
    total[...] = jnp.zeros_like(total)
    for y in range(Y):
        row = grad_ref[y].astype(jnp.float32)
        whole = jnp.concatenate([shifted(row, 1 - b) for b in range(3)], axis=0)
        stack[:, y * X : (y + 1) * X] = whole.astype(jnp.bfloat16)
    mix = jnp.concatenate(
        [
            jnp.concatenate(
                [weight_ref[3 * a + b].astype(jnp.float32).T for b in range(3)], axis=1
            )
            for a in range(3)
        ],
        axis=0,
    ).astype(jnp.bfloat16)
    for j in range(Y // 2):
        at = j * 2 * X
        part = jnp.dot(mix, stack[:, at : at + 2 * X], preferred_element_type=jnp.float32)
        for a in range(3):
            place = slice(at + a * X, at + (a + 2) * X)
            total[:, place] += part[a * C : (a + 1) * C]
    for y in range(Y):
        conv = total[:, (y + 1) * X : (y + 2) * X]
        out_ref[y] = (g_ref[y].astype(jnp.float32) + conv).astype(jnp.bfloat16)


def turn_kernel(own_ref, other_ref, rows_ref, last_ref):
    for slot, raw_ref in enumerate((own_ref, other_ref)):
        rows = jnp.swapaxes(raw_ref[...].astype(jnp.float32), 0, 1).astype(jnp.bfloat16)
        rows_ref[slot] = rows
        last_ref[slot] = rows[3]


def blur_kernel(half_ref, taps_ref, rows_ref, halo_ref, out_ref):
    half = half_ref[0]
    for slot, place in enumerate((half, 1 - half)):
        before = halo_ref[slot].astype(jnp.float32)
        for k in range(4):
            row = rows_ref[slot, k].astype(jnp.float32)
            for pair in range(4):
                value = taps_ref[pair : pair + 1] * row
                if pair == 0:
                    value = value + taps_ref[4:5] * before
                out_ref[4 * k + pair, place] = value.astype(jnp.bfloat16)
            before = row


def unpack_kernel(whole_ref, weight_ref, bias_ref):
    top, bottom = (
        jnp.concatenate(
            [whole_ref[half * C // PIECE + piece] for piece in range(C // PIECE)], axis=0
        )
        for half in range(2)
    )
    rows = (
        (top, 0),
        (top, 1),
        (bottom, 2),
        (bottom, 0),
        (bottom, 1),
        (bottom, 3),
        (top, 2),
        (top, 3),
        (top, 4),
    )
    for tap, (block, place) in enumerate(rows):
        weight_ref[tap] = block[:, place * C : (place + 1) * C]
    bias_ref[...] = bottom[0:1, 4 * C : 5 * C]


def spread_sum_kernel(parts_ref, out_ref):
    total = jnp.sum(parts_ref[...], axis=0)
    for copy in range(out_ref.shape[0]):
        out_ref[copy] = total


def scaled_sum_kernel(factor, parts_ref, out_ref):
    total = jnp.sum(parts_ref[...], axis=0) * factor
    for copy in range(out_ref.shape[0]):
        out_ref[copy] = total


def call(kernel, outs, scratch, flops, moved, *args, scalars=0, far=0):
    return pl.pallas_call(
        kernel,
        out_shape=outs,
        in_specs=[pl.BlockSpec(memory_space=pltpu.SMEM)] * scalars
        + [pl.BlockSpec(memory_space=pltpu.VMEM)] * (len(args) - scalars - far)
        + [pl.BlockSpec(memory_space=pltpu.HBM)] * far,
        out_specs=jax.tree.map(lambda _: pl.BlockSpec(memory_space=pltpu.VMEM), outs),
        scratch_shapes=scratch,
        compiler_params=pltpu.CompilerParams(vmem_limit_bytes=VMEM_LIMIT),
        cost_estimate=pl.CostEstimate(flops=flops, bytes_accessed=moved, transcendentals=0),
    )(*args)


def on_device(activations, cotangent, weight, conv_bias, blur_taps):
    shape = jax.ShapeDtypeStruct
    bf16, f32 = jnp.bfloat16, jnp.float32
    raw = cotangent[:, :, 0, :]
    other = lax.ppermute(raw, "zh", [(0, 1), (1, 0)])
    half = lax.axis_index("zh").astype(jnp.int32)[None]
    flops = 2 * Y * X * 9 * C * C
    slope, turned, coef = call(
        forward_kernel,
        (shape((Y, C, X), f32), shape((Y * X, WIDE), bf16), shape((8, X), f32)),
        [
            pltpu.VMEM((3 * C, Y * X), bf16),
            pltpu.VMEM((C, (Y + 2) * X), f32),
            pltpu.VMEM((C, Y, X), bf16),
            pltpu.VMEM((9, C, C), bf16),
            pltpu.SemaphoreType.DMA((2,)),
        ],
        64 * flops,
        128 << 20,
        half,
        blur_taps,
        conv_bias[None, :],
        activations[:, 0],
        weight,
        scalars=2,
        far=2,
    )
    slope, turned, coef, raw = lax.optimization_barrier((slope, turned, coef, raw))
    rows, last = call(
        turn_kernel,
        (shape((2, 4, C, X), bf16), shape((2, C, X), bf16)),
        [],
        1 << 16,
        1 << 18,
        raw,
        other,
    )
    hops = [
        ((group * N_CROSS + cross) * 2, ((group + 1) * N_CROSS + cross) * 2)
        for group in range(N_GROUP - 1)
        for cross in range(N_CROSS)
    ]
    halo = lax.ppermute(last, AXES, hops)
    field = call(
        blur_kernel,
        shape((N_CROSS, 2, C, X), bf16),
        [],
        1 << 20,
        1 << 20,
        half,
        coef,
        rows,
        halo,
        scalars=1,
    )
    g_out = lax.all_to_all(field, CROSS, 0, 0, tiled=True).reshape(Y, C, X)
    grad, sums = call(
        weight_kernel,
        (shape((Y, C, X), bf16), shape((N_FLAT, PIECE, LONG), f32)),
        [pltpu.VMEM((3 * C, Y * X), bf16)],
        flops,
        4 << 20,
        g_out,
        slope,
        turned,
    )
    out = call(
        input_kernel,
        shape((Y, C, X), bf16),
        [pltpu.VMEM((3 * C, Y * X), bf16), pltpu.VMEM((C, (Y + 2) * X), f32)],
        flops,
        2 << 20,
        grad,
        g_out,
        weight,
    )
    grad_input = out.transpose(1, 0, 2)[:, None]

    parts = lax.all_to_all(sums, FLAT, 0, 0, tiled=True)
    sent = call(
        spread_sum_kernel, shape((N_COLUMN, PIECE, LONG), f32), [], 1 << 16, 1 << 18, parts
    )
    columns = [
        [
            (((z % 8) * 2 + core) * N_CROSS + cross) * 2 + z // 8
            for z in [(FIRST + step) % N_COLUMN for step in range(N_COLUMN)]
        ]
        for core in range(2)
        for cross in range(N_CROSS)
    ]
    parts = lax.all_to_all(sent, AXES, 0, 0, axis_index_groups=columns, tiled=True)
    parts, grad_input = lax.optimization_barrier((parts, grad_input))
    factor = float(512 * Y * X) ** -0.5
    sent = call(
        lambda a, b: scaled_sum_kernel(factor, a, b),
        shape((N_FLAT, PIECE, LONG), f32),
        [],
        1 << 16,
        1 << 18,
        parts,
    )
    whole = lax.all_to_all(sent, FLAT, 0, 0, tiled=True)
    grad_w, grad_b = call(
        unpack_kernel, (shape((9, C, C), f32), shape((1, C), f32)), [], 1, 1 << 18, whole
    )
    return grad_input, grad_w, grad_b.reshape(C)


def solution(mesh):
    fine = Mesh(mesh.devices.reshape(SIZES), AXES)
    in_specs = (P(None, AXES, None, None), P(None, GROUP, PLANE, None), P(), P(), P())
    out_specs = (P(None, AXES, None, None), P(), P())
    return jax.shard_map(
        on_device, mesh=fine, in_specs=in_specs, out_specs=out_specs, check_vma=False
    )
```

```python
import jax
import jax.numpy as jnp
from jax import lax
from jax.experimental import pallas as pl
from jax.experimental.pallas import tpu as pltpu
from jax.sharding import Mesh
from jax.sharding import PartitionSpec as P

R = 8
C = 64
Y = 32
X = 128
AXES = ("zl", "core", "x", "y", "zh")
SIZES = (8, 2, 4, 4, 2)
GROUP = ("zl", "core")
PLANE = ("x", "y", "zh")
N_CROSS = 16
N_FLAT = 32
N_GROUP = 16
N_COLUMN = 16
FIRST = 6
PIECE = 4
LONG = 384
WIDE = 256
VMEM_LIMIT = 16 * 1024 * 1024
CORNER = 3
CROSS_ORDER = [
    ((CORNER + a) % 4, (CORNER + b) % 4) for a in range(4) for b in range(4)
]
PLACE = [CROSS_ORDER.index((y // 8, y // 2 % 4)) * 2 + y % 2 for y in range(Y)]


def shifted(row, step):
    if step == 0:
        return row
    lane = lax.broadcasted_iota(jnp.int32, row.shape, 1)
    edge = 0 if step < 0 else X - 1
    return jnp.where(lane == edge, 0.0, pltpu.roll(row, (-step) % X, 1))


def forward_kernel(
    half_ref,
    taps_ref,
    bias_ref,
    act_far,
    weight_far,
    slope_ref,
    turned_ref,
    coef_ref,
    stack,
    hidden,
    act_ref,
    weight_ref,
    sems,
):
    copies = [
        pltpu.make_async_copy(act_far, act_ref, sems.at[0]),
        pltpu.make_async_copy(weight_far, weight_ref, sems.at[1]),
    ]
    for copy in copies:
        copy.start()
    half = half_ref[0]
    for pair in range(4):
        coef_ref[pair : pair + 1] = jnp.full((1, X), taps_ref[2 * pair + half], jnp.float32)
    spill = jnp.where(half == 0, taps_ref[R], 0.0)
    coef_ref[4:] = jnp.full((4, X), spill, jnp.float32)
    column = lax.broadcasted_iota(jnp.int32, (X, WIDE - 3 * C), 1)
    ones = jnp.where(column == 0, 1.0, 0.0).astype(jnp.bfloat16)
    for copy in copies:
        copy.wait()
    for y in range(Y):
        if y % 16 == 0:
            rows = jnp.swapaxes(act_ref[:, y : y + 16].astype(jnp.float32), 0, 1)
        row = rows[y % 16]
        at = slice(y * X, (y + 1) * X)
        whole = jnp.concatenate([shifted(row, b - 1) for b in range(3)], axis=0)
        stack[:, at] = whole.astype(jnp.bfloat16)
        turned_ref[at, : 3 * C] = whole.T.astype(jnp.bfloat16)
        turned_ref[at, 3 * C :] = ones
    square = (C, C)
    diagonal = lax.broadcasted_iota(jnp.int32, square, 0) == lax.broadcasted_iota(
        jnp.int32, square, 1
    )
    bias = jnp.sum(jnp.where(diagonal, bias_ref[...], 0.0), axis=1, keepdims=True)
    hidden[...] = jnp.broadcast_to(bias, hidden.shape)
    mix = jnp.concatenate(
        [jnp.concatenate([weight_ref[3 * a + b] for b in range(3)], axis=1) for a in range(3)],
        axis=0,
    )
    for j in range(Y // 2):
        at = j * 2 * X
        part = jnp.dot(mix, stack[:, at : at + 2 * X], preferred_element_type=jnp.float32)
        for a in range(3):
            place = slice(at + (2 - a) * X, at + (4 - a) * X)
            hidden[:, place] += part[a * C : (a + 1) * C]
    for y in range(Y):
        h = hidden[:, (y + 1) * X : (y + 2) * X]
        s = jax.nn.sigmoid(h)
        slope_ref[y] = s * (1.0 + h * (1.0 - s))


def weight_kernel(g_ref, slope_ref, turned_ref, grad_ref, sums_ref, stack):
    zero = jnp.zeros((C, X), jnp.bfloat16)
    stack[0:C, (Y - 1) * X :] = zero
    stack[2 * C :, 0:X] = zero
    for y in range(Y):
        grad = (g_ref[PLACE[y]].astype(jnp.float32) * slope_ref[y]).astype(jnp.bfloat16)
        grad_ref[y] = grad
        for a in range(3):
            row = y + a - 1
            if 0 <= row < Y:
                stack[a * C : (a + 1) * C, row * X : (row + 1) * X] = grad
    total = jnp.zeros((3 * C, WIDE), jnp.float32)
    for j in range(Y // 2):
        at = slice(j * 2 * X, (j + 1) * 2 * X)
        total += jnp.dot(stack[:, at], turned_ref[at, :], preferred_element_type=jnp.float32)
    square = (C, C)
    diagonal = lax.broadcasted_iota(jnp.int32, square, 0) == lax.broadcasted_iota(
        jnp.int32, square, 1
    )
    bias = total[C : 2 * C, 3 * C : 3 * C + 1]
    row = jnp.sum(jnp.where(diagonal, bias, 0.0), axis=0, keepdims=True)
    first = lax.broadcasted_iota(jnp.int32, square, 0) == 0
    zero = jnp.zeros(square, jnp.float32)
    sides = [total[a * C : (a + 1) * C, 2 * C : 3 * C] for a in range(3)]
    low = jnp.concatenate([sides[0], sides[1]], axis=1)
    high = jnp.concatenate([sides[2], zero], axis=1)
    last = jnp.concatenate([jnp.where(first, row, 0.0), zero], axis=1)
    top = jnp.concatenate([total[:C, : 2 * C], total[2 * C :, : 2 * C], high], axis=1)
    bottom = jnp.concatenate([total[C : 2 * C, : 2 * C], low, last], axis=1)
    for half, block in enumerate((top, bottom)):
        for piece in range(C // PIECE):
            sums_ref[half * C // PIECE + piece] = block[piece * PIECE : (piece + 1) * PIECE]


def input_kernel(grad_ref, g_ref, weight_ref, out_ref, stack, total):
    total[...] = jnp.zeros_like(total)
    for y in range(Y):
        row = grad_ref[y].astype(jnp.float32)
        whole = jnp.concatenate([shifted(row, 1 - b) for b in range(3)], axis=0)
        stack[:, y * X : (y + 1) * X] = whole.astype(jnp.bfloat16)
    mix = jnp.concatenate(
        [
            jnp.concatenate(
                [weight_ref[3 * a + b].astype(jnp.float32).T for b in range(3)], axis=1
            )
            for a in range(3)
        ],
        axis=0,
    ).astype(jnp.bfloat16)
    for j in range(Y // 2):
        at = j * 2 * X
        part = jnp.dot(mix, stack[:, at : at + 2 * X], preferred_element_type=jnp.float32)
        for a in range(3):
            place = slice(at + a * X, at + (a + 2) * X)
            total[:, place] += part[a * C : (a + 1) * C]
    for y in range(0, Y, 16):
        rows = []
        for row in range(y, y + 16):
            conv = total[:, (row + 1) * X : (row + 2) * X]
            rows.append(g_ref[PLACE[row]].astype(jnp.float32) + conv)
        turned = jnp.swapaxes(jnp.stack(rows), 0, 1)
        out_ref[:, y : y + 16] = turned.astype(jnp.bfloat16)


def turn_kernel(own_ref, other_ref, rows_ref, last_ref):
    for slot, raw_ref in enumerate((own_ref, other_ref)):
        rows = jnp.swapaxes(raw_ref[...].astype(jnp.float32), 0, 1).astype(jnp.bfloat16)
        rows_ref[slot] = rows
        last_ref[slot] = rows[3]


def blur_kernel(half_ref, taps_ref, rows_ref, halo_ref, out_ref):
    half = half_ref[0]
    for slot, place in enumerate((half, 1 - half)):
        before = halo_ref[slot].astype(jnp.float32)
        for k in range(4):
            row = rows_ref[slot, k].astype(jnp.float32)
            for pair in range(4):
                value = taps_ref[pair : pair + 1] * row
                if pair == 0:
                    value = value + taps_ref[4:5] * before
                out_ref[CROSS_ORDER.index((k, pair)), place] = value.astype(jnp.bfloat16)
            before = row


def unpack_kernel(whole_ref, weight_ref, bias_ref):
    top, bottom = (
        jnp.concatenate(
            [whole_ref[half * C // PIECE + piece] for piece in range(C // PIECE)], axis=0
        )
        for half in range(2)
    )
    rows = (
        (top, 0),
        (top, 1),
        (bottom, 2),
        (bottom, 0),
        (bottom, 1),
        (bottom, 3),
        (top, 2),
        (top, 3),
        (top, 4),
    )
    for tap, (block, place) in enumerate(rows):
        weight_ref[tap] = block[:, place * C : (place + 1) * C]
    bias_ref[...] = bottom[0:1, 4 * C : 5 * C]


def spread_sum_kernel(parts_ref, out_ref):
    total = jnp.sum(parts_ref[...], axis=0)
    for copy in range(out_ref.shape[0]):
        out_ref[copy] = total


def scaled_sum_kernel(factor, parts_ref, out_ref):
    total = jnp.sum(parts_ref[...], axis=0) * factor
    for copy in range(out_ref.shape[0]):
        out_ref[copy] = total


def call(kernel, outs, scratch, flops, moved, *args, scalars=0, far=0):
    return pl.pallas_call(
        kernel,
        out_shape=outs,
        in_specs=[pl.BlockSpec(memory_space=pltpu.SMEM)] * scalars
        + [pl.BlockSpec(memory_space=pltpu.VMEM)] * (len(args) - scalars - far)
        + [pl.BlockSpec(memory_space=pltpu.HBM)] * far,
        out_specs=jax.tree.map(lambda _: pl.BlockSpec(memory_space=pltpu.VMEM), outs),
        scratch_shapes=scratch,
        compiler_params=pltpu.CompilerParams(vmem_limit_bytes=VMEM_LIMIT),
        cost_estimate=pl.CostEstimate(flops=flops, bytes_accessed=moved, transcendentals=0),
    )(*args)


def on_device(activations, cotangent, weight, conv_bias, blur_taps):
    shape = jax.ShapeDtypeStruct
    bf16, f32 = jnp.bfloat16, jnp.float32
    raw = cotangent[:, :, 0, :]
    other = lax.ppermute(raw, "zh", [(0, 1), (1, 0)])
    half = lax.axis_index("zh").astype(jnp.int32)[None]
    flops = 2 * Y * X * 9 * C * C
    slope, turned, coef = call(
        forward_kernel,
        (shape((Y, C, X), f32), shape((Y * X, WIDE), bf16), shape((8, X), f32)),
        [
            pltpu.VMEM((3 * C, Y * X), bf16),
            pltpu.VMEM((C, (Y + 2) * X), f32),
            pltpu.VMEM((C, Y, X), bf16),
            pltpu.VMEM((9, C, C), bf16),
            pltpu.SemaphoreType.DMA((2,)),
        ],
        64 * flops,
        128 << 20,
        half,
        blur_taps,
        conv_bias[None, :],
        activations[:, 0],
        weight,
        scalars=2,
        far=2,
    )
    slope, turned, coef, raw = lax.optimization_barrier((slope, turned, coef, raw))
    rows, last = call(
        turn_kernel,
        (shape((2, 4, C, X), bf16), shape((2, C, X), bf16)),
        [],
        1 << 16,
        1 << 18,
        raw,
        other,
    )
    hops = [
        ((group * N_CROSS + cross) * 2, ((group + 1) * N_CROSS + cross) * 2)
        for group in range(N_GROUP - 1)
        for cross in range(N_CROSS)
    ]
    halo = lax.ppermute(last, AXES, hops)
    field = call(
        blur_kernel,
        shape((N_CROSS, 2, C, X), bf16),
        [],
        1 << 20,
        1 << 20,
        half,
        coef,
        rows,
        halo,
        scalars=1,
    )
    crosses = [
        [(group * 4 + x) * 8 + y * 2 + zh for x, y in CROSS_ORDER]
        for group in range(N_GROUP)
        for zh in range(2)
    ]
    g_out = lax.all_to_all(field, AXES, 0, 0, axis_index_groups=crosses, tiled=True)
    g_out = g_out.reshape(Y, C, X)
    grad, sums = call(
        weight_kernel,
        (shape((Y, C, X), bf16), shape((N_FLAT, PIECE, LONG), f32)),
        [pltpu.VMEM((3 * C, Y * X), bf16)],
        flops,
        4 << 20,
        g_out,
        slope,
        turned,
    )
    grad_input = call(
        input_kernel,
        shape((C, Y, X), bf16),
        [pltpu.VMEM((3 * C, Y * X), bf16), pltpu.VMEM((C, (Y + 2) * X), f32)],
        flops,
        2 << 20,
        grad,
        g_out,
        weight,
    )

    flats = [
        [((zl * 2 + core) * 4 + x) * 8 + y * 2 + zh for core in range(2) for x, y in CROSS_ORDER]
        for zl in range(8)
        for zh in range(2)
    ]
    parts = lax.all_to_all(sums, AXES, 0, 0, axis_index_groups=flats, tiled=True)
    sent = call(
        spread_sum_kernel, shape((N_COLUMN, PIECE, LONG), f32), [], 1 << 16, 1 << 18, parts
    )
    columns = [
        [
            (((z % 8) * 2 + core) * N_CROSS + cross) * 2 + z // 8
            for z in [(FIRST + step) % N_COLUMN for step in range(N_COLUMN)]
        ]
        for core in range(2)
        for cross in range(N_CROSS)
    ]
    parts = lax.all_to_all(sent, AXES, 0, 0, axis_index_groups=columns, tiled=True)
    parts, grad_input = lax.optimization_barrier((parts, grad_input))
    factor = float(512 * Y * X) ** -0.5
    sent = call(
        lambda a, b: scaled_sum_kernel(factor, a, b),
        shape((N_FLAT, PIECE, LONG), f32),
        [],
        1 << 16,
        1 << 18,
        parts,
    )
    whole = lax.all_to_all(sent, AXES, 0, 0, axis_index_groups=flats, tiled=True)
    grad_w, grad_b = call(
        unpack_kernel, (shape((9, C, C), f32), shape((1, C), f32)), [], 1, 1 << 18, whole
    )
    return grad_input[:, None], grad_w, grad_b.reshape(C)


def solution(mesh):
    fine = Mesh(mesh.devices.reshape(SIZES), AXES)
    in_specs = (P(None, AXES, None, None), P(None, GROUP, PLANE, None), P(), P(), P())
    out_specs = (P(None, AXES, None, None), P(), P())
    return jax.shard_map(
        on_device, mesh=fine, in_specs=in_specs, out_specs=out_specs, check_vma=False
    )
```

```python
import jax
import jax.numpy as jnp
from jax import lax
from jax.experimental import pallas as pl
from jax.experimental.pallas import tpu as pltpu
from jax.sharding import Mesh
from jax.sharding import PartitionSpec as P

R = 8
C = 64
Y = 32
X = 128
AXES = ("zl", "core", "x", "y", "zh")
SIZES = (8, 2, 4, 4, 2)
GROUP = ("zl", "core")
PLANE = ("x", "y", "zh")
N_CROSS = 16
N_FLAT = 32
N_GROUP = 16
N_COLUMN = 16
FIRST = 6
PIECE = 2
LONG = 640
WIDE = 256
VMEM_LIMIT = 16 * 1024 * 1024
CORNER = 3
CROSS_ORDER = [
    ((CORNER + a) % 4, (CORNER + b) % 4) for a in range(4) for b in range(4)
]
PLACE = [CROSS_ORDER.index((y // 8, y // 2 % 4)) * 2 + y % 2 for y in range(Y)]


def shifted(row, step):
    if step == 0:
        return row
    lane = lax.broadcasted_iota(jnp.int32, row.shape, 1)
    edge = 0 if step < 0 else X - 1
    return jnp.where(lane == edge, 0.0, pltpu.roll(row, (-step) % X, 1))


def forward_kernel(
    half_ref,
    taps_ref,
    bias_ref,
    act_far,
    weight_far,
    slope_ref,
    turned_ref,
    coef_ref,
    stack,
    hidden,
    act_ref,
    weight_ref,
    sems,
):
    copies = [
        pltpu.make_async_copy(act_far, act_ref, sems.at[0]),
        pltpu.make_async_copy(weight_far, weight_ref, sems.at[1]),
    ]
    for copy in copies:
        copy.start()
    half = half_ref[0]
    for pair in range(4):
        coef_ref[pair : pair + 1] = jnp.full((1, X), taps_ref[2 * pair + half], jnp.float32)
    spill = jnp.where(half == 0, taps_ref[R], 0.0)
    coef_ref[4:] = jnp.full((4, X), spill, jnp.float32)
    column = lax.broadcasted_iota(jnp.int32, (X, WIDE - 3 * C), 1)
    ones = jnp.where(column == 0, 1.0, 0.0).astype(jnp.bfloat16)
    for copy in copies:
        copy.wait()
    for y in range(Y):
        if y % 16 == 0:
            rows = jnp.swapaxes(act_ref[:, y : y + 16].astype(jnp.float32), 0, 1)
        row = rows[y % 16]
        at = slice(y * X, (y + 1) * X)
        whole = jnp.concatenate([shifted(row, b - 1) for b in range(3)], axis=0)
        stack[:, at] = whole.astype(jnp.bfloat16)
        turned_ref[at, : 3 * C] = whole.T.astype(jnp.bfloat16)
        turned_ref[at, 3 * C :] = ones
    square = (C, C)
    diagonal = lax.broadcasted_iota(jnp.int32, square, 0) == lax.broadcasted_iota(
        jnp.int32, square, 1
    )
    bias = jnp.sum(jnp.where(diagonal, bias_ref[...], 0.0), axis=1, keepdims=True)
    hidden[...] = jnp.broadcast_to(bias, hidden.shape)
    mix = jnp.concatenate(
        [jnp.concatenate([weight_ref[3 * a + b] for b in range(3)], axis=1) for a in range(3)],
        axis=0,
    )
    for j in range(Y // 2):
        at = j * 2 * X
        part = jnp.dot(mix, stack[:, at : at + 2 * X], preferred_element_type=jnp.float32)
        for a in range(3):
            place = slice(at + (2 - a) * X, at + (4 - a) * X)
            hidden[:, place] += part[a * C : (a + 1) * C]
    for y in range(Y):
        h = hidden[:, (y + 1) * X : (y + 2) * X]
        s = jax.nn.sigmoid(h)
        slope_ref[y] = s * (1.0 + h * (1.0 - s))


def weight_kernel(g_ref, slope_ref, turned_ref, grad_ref, sums_ref, stack):
    zero = jnp.zeros((C, X), jnp.bfloat16)
    stack[0:C, (Y - 1) * X :] = zero
    stack[2 * C :, 0:X] = zero
    for y in range(Y):
        grad = (g_ref[PLACE[y]].astype(jnp.float32) * slope_ref[y]).astype(jnp.bfloat16)
        grad_ref[y] = grad
        for a in range(3):
            row = y + a - 1
            if 0 <= row < Y:
                stack[a * C : (a + 1) * C, row * X : (row + 1) * X] = grad
    total = jnp.zeros((3 * C, WIDE), jnp.float32)
    for j in range(Y // 2):
        at = slice(j * 2 * X, (j + 1) * 2 * X)
        total += jnp.dot(stack[:, at], turned_ref[at, :], preferred_element_type=jnp.float32)
    square = (C, C)
    diagonal = lax.broadcasted_iota(jnp.int32, square, 0) == lax.broadcasted_iota(
        jnp.int32, square, 1
    )
    bias = total[C : 2 * C, 3 * C : 3 * C + 1]
    row = jnp.sum(jnp.where(diagonal, bias, 0.0), axis=0, keepdims=True)
    first = lax.broadcasted_iota(jnp.int32, square, 0) == 0
    last = jnp.where(first, row, 0.0)
    blocks = [
        total[a * C : (a + 1) * C, b * C : (b + 1) * C] for a in range(3) for b in range(3)
    ]
    whole = jnp.concatenate(blocks + [last], axis=1)
    for piece in range(N_FLAT):
        sums_ref[piece] = whole[piece * PIECE : (piece + 1) * PIECE]


def input_kernel(grad_ref, g_ref, weight_ref, out_ref, stack, total):
    total[...] = jnp.zeros_like(total)
    for y in range(Y):
        row = grad_ref[y].astype(jnp.float32)
        whole = jnp.concatenate([shifted(row, 1 - b) for b in range(3)], axis=0)
        stack[:, y * X : (y + 1) * X] = whole.astype(jnp.bfloat16)
    mix = jnp.concatenate(
        [
            jnp.concatenate(
                [weight_ref[3 * a + b].astype(jnp.float32).T for b in range(3)], axis=1
            )
            for a in range(3)
        ],
        axis=0,
    ).astype(jnp.bfloat16)
    for j in range(Y // 2):
        at = j * 2 * X
        part = jnp.dot(mix, stack[:, at : at + 2 * X], preferred_element_type=jnp.float32)
        for a in range(3):
            place = slice(at + a * X, at + (a + 2) * X)
            total[:, place] += part[a * C : (a + 1) * C]
    for y in range(0, Y, 16):
        rows = []
        for row in range(y, y + 16):
            conv = total[:, (row + 1) * X : (row + 2) * X]
            rows.append(g_ref[PLACE[row]].astype(jnp.float32) + conv)
        turned = jnp.swapaxes(jnp.stack(rows), 0, 1)
        out_ref[:, y : y + 16] = turned.astype(jnp.bfloat16)


def turn_kernel(own_ref, other_ref, rows_ref, last_ref):
    for slot, raw_ref in enumerate((own_ref, other_ref)):
        rows = jnp.swapaxes(raw_ref[...].astype(jnp.float32), 0, 1).astype(jnp.bfloat16)
        rows_ref[slot] = rows
        last_ref[slot] = rows[3]


def blur_kernel(half_ref, taps_ref, rows_ref, halo_ref, out_ref):
    half = half_ref[0]
    for slot, place in enumerate((half, 1 - half)):
        before = halo_ref[slot].astype(jnp.float32)
        for k in range(4):
            row = rows_ref[slot, k].astype(jnp.float32)
            for pair in range(4):
                value = taps_ref[pair : pair + 1] * row
                if pair == 0:
                    value = value + taps_ref[4:5] * before
                out_ref[CROSS_ORDER.index((k, pair)), place] = value.astype(jnp.bfloat16)
            before = row


def unpack_kernel(whole_ref, weight_ref, bias_ref):
    whole = jnp.concatenate([whole_ref[piece] for piece in range(N_FLAT)], axis=0)
    for tap in range(9):
        weight_ref[tap] = whole[:, tap * C : (tap + 1) * C]
    bias_ref[...] = whole[0:1, 9 * C :]


def spread_sum_kernel(parts_ref, out_ref):
    total = jnp.sum(parts_ref[...], axis=0)
    for copy in range(out_ref.shape[0]):
        out_ref[copy] = total


def scaled_sum_kernel(factor, parts_ref, out_ref):
    total = jnp.sum(parts_ref[...], axis=0) * factor
    for copy in range(out_ref.shape[0]):
        out_ref[copy] = total


def call(kernel, outs, scratch, flops, moved, *args, scalars=0, far=0):
    return pl.pallas_call(
        kernel,
        out_shape=outs,
        in_specs=[pl.BlockSpec(memory_space=pltpu.SMEM)] * scalars
        + [pl.BlockSpec(memory_space=pltpu.VMEM)] * (len(args) - scalars - far)
        + [pl.BlockSpec(memory_space=pltpu.HBM)] * far,
        out_specs=jax.tree.map(lambda _: pl.BlockSpec(memory_space=pltpu.VMEM), outs),
        scratch_shapes=scratch,
        compiler_params=pltpu.CompilerParams(vmem_limit_bytes=VMEM_LIMIT),
        cost_estimate=pl.CostEstimate(flops=flops, bytes_accessed=moved, transcendentals=0),
    )(*args)


def on_device(activations, cotangent, weight, conv_bias, blur_taps):
    shape = jax.ShapeDtypeStruct
    bf16, f32 = jnp.bfloat16, jnp.float32
    raw = cotangent[:, :, 0, :]
    other = lax.ppermute(raw, "zh", [(0, 1), (1, 0)])
    half = lax.axis_index("zh").astype(jnp.int32)[None]
    flops = 2 * Y * X * 9 * C * C
    slope, turned, coef = call(
        forward_kernel,
        (shape((Y, C, X), f32), shape((Y * X, WIDE), bf16), shape((8, X), f32)),
        [
            pltpu.VMEM((3 * C, Y * X), bf16),
            pltpu.VMEM((C, (Y + 2) * X), f32),
            pltpu.VMEM((C, Y, X), bf16),
            pltpu.VMEM((9, C, C), bf16),
            pltpu.SemaphoreType.DMA((2,)),
        ],
        64 * flops,
        128 << 20,
        half,
        blur_taps,
        conv_bias[None, :],
        activations[:, 0],
        weight,
        scalars=2,
        far=2,
    )
    slope, turned, coef, raw = lax.optimization_barrier((slope, turned, coef, raw))
    rows, last = call(
        turn_kernel,
        (shape((2, 4, C, X), bf16), shape((2, C, X), bf16)),
        [],
        1 << 16,
        1 << 18,
        raw,
        other,
    )
    hops = [
        ((group * N_CROSS + cross) * 2, ((group + 1) * N_CROSS + cross) * 2)
        for group in range(N_GROUP - 1)
        for cross in range(N_CROSS)
    ]
    halo = lax.ppermute(last, AXES, hops)
    field = call(
        blur_kernel,
        shape((N_CROSS, 2, C, X), bf16),
        [],
        1 << 20,
        1 << 20,
        half,
        coef,
        rows,
        halo,
        scalars=1,
    )
    crosses = [
        [(group * 4 + x) * 8 + y * 2 + zh for x, y in CROSS_ORDER]
        for group in range(N_GROUP)
        for zh in range(2)
    ]
    g_out = lax.all_to_all(field, AXES, 0, 0, axis_index_groups=crosses, tiled=True)
    g_out = g_out.reshape(Y, C, X)
    grad, sums = call(
        weight_kernel,
        (shape((Y, C, X), bf16), shape((N_FLAT, PIECE, LONG), f32)),
        [pltpu.VMEM((3 * C, Y * X), bf16)],
        flops,
        4 << 20,
        g_out,
        slope,
        turned,
    )
    grad_input = call(
        input_kernel,
        shape((C, Y, X), bf16),
        [pltpu.VMEM((3 * C, Y * X), bf16), pltpu.VMEM((C, (Y + 2) * X), f32)],
        flops,
        2 << 20,
        grad,
        g_out,
        weight,
    )

    flats = [
        [((zl * 2 + core) * 4 + x) * 8 + y * 2 + zh for core in range(2) for x, y in CROSS_ORDER]
        for zl in range(8)
        for zh in range(2)
    ]
    parts = lax.all_to_all(sums, AXES, 0, 0, axis_index_groups=flats, tiled=True)
    sent = call(
        spread_sum_kernel, shape((N_COLUMN, PIECE, LONG), f32), [], 1 << 16, 1 << 18, parts
    )
    columns = [
        [
            (((z % 8) * 2 + core) * N_CROSS + cross) * 2 + z // 8
            for z in [(FIRST + step) % N_COLUMN for step in range(N_COLUMN)]
        ]
        for core in range(2)
        for cross in range(N_CROSS)
    ]
    parts = lax.all_to_all(sent, AXES, 0, 0, axis_index_groups=columns, tiled=True)
    parts, grad_input = lax.optimization_barrier((parts, grad_input))
    factor = float(512 * Y * X) ** -0.5
    sent = call(
        lambda a, b: scaled_sum_kernel(factor, a, b),
        shape((N_FLAT, PIECE, LONG), f32),
        [],
        1 << 16,
        1 << 18,
        parts,
    )
    whole = lax.all_to_all(sent, AXES, 0, 0, axis_index_groups=flats, tiled=True)
    grad_w, grad_b = call(
        unpack_kernel, (shape((9, C, C), f32), shape((1, C), f32)), [], 1, 1 << 18, whole
    )
    return grad_input[:, None], grad_w, grad_b.reshape(C)


def solution(mesh):
    fine = Mesh(mesh.devices.reshape(SIZES), AXES)
    in_specs = (P(None, AXES, None, None), P(None, GROUP, PLANE, None), P(), P(), P())
    out_specs = (P(None, AXES, None, None), P(), P())
    return jax.shard_map(
        on_device, mesh=fine, in_specs=in_specs, out_specs=out_specs, check_vma=False
    )
```

```python
import jax
import jax.numpy as jnp
from jax import lax
from jax.experimental import pallas as pl
from jax.experimental.pallas import tpu as pltpu
from jax.sharding import Mesh
from jax.sharding import PartitionSpec as P

R = 8
C = 64
Y = 32
X = 128
AXES = ("zl", "core", "x", "y", "zh")
SIZES = (8, 2, 4, 4, 2)
GROUP = ("zl", "core")
PLANE = ("x", "y", "zh")
N_CROSS = 16
N_FLAT = 32
N_GROUP = 16
N_COLUMN = 16
FIRST = 7
PIECE = 2
LONG = 640
WIDE = 256
VMEM_LIMIT = 16 * 1024 * 1024
CORNER = 3
CROSS_ORDER = [
    ((CORNER + a) % 4, (CORNER + b) % 4) for a in range(4) for b in range(4)
]
PLACE = [CROSS_ORDER.index((y // 8, y // 2 % 4)) * 2 + y % 2 for y in range(Y)]


def shifted(row, step):
    if step == 0:
        return row
    lane = lax.broadcasted_iota(jnp.int32, row.shape, 1)
    edge = 0 if step < 0 else X - 1
    return jnp.where(lane == edge, 0.0, pltpu.roll(row, (-step) % X, 1))


def forward_kernel(
    half_ref,
    taps_far,
    bias_far,
    act_far,
    weight_far,
    slope_ref,
    turned_ref,
    coef_ref,
    stack,
    hidden,
    taps_ref,
    bias_ref,
    act_ref,
    weight_ref,
    sems,
):
    fars = (taps_far, bias_far, act_far, weight_far)
    nears = (taps_ref, bias_ref, act_ref, weight_ref)
    copies = [
        pltpu.make_async_copy(far, near, sems.at[i])
        for i, (far, near) in enumerate(zip(fars, nears))
    ]
    for copy in copies:
        copy.start()
    for copy in copies:
        copy.wait()
    low = half_ref[0] == 0
    for pair in range(4):
        even, odd = (taps_ref[:, 2 * pair + i : 2 * pair + i + 1] for i in range(2))
        coef_ref[pair : pair + 1] = jnp.broadcast_to(jnp.where(low, even, odd), (1, X))
    spill = jnp.where(low, taps_ref[:, R : R + 1], 0.0)
    coef_ref[4:] = jnp.broadcast_to(spill, (4, X))
    column = lax.broadcasted_iota(jnp.int32, (X, WIDE - 3 * C), 1)
    ones = jnp.where(column == 0, 1.0, 0.0).astype(jnp.bfloat16)
    for y in range(Y):
        if y % 16 == 0:
            rows = jnp.swapaxes(act_ref[:, y : y + 16].astype(jnp.float32), 0, 1)
        row = rows[y % 16]
        at = slice(y * X, (y + 1) * X)
        whole = jnp.concatenate([shifted(row, b - 1) for b in range(3)], axis=0)
        stack[:, at] = whole.astype(jnp.bfloat16)
        turned_ref[at, : 3 * C] = whole.T.astype(jnp.bfloat16)
        turned_ref[at, 3 * C :] = ones
    square = (C, C)
    diagonal = lax.broadcasted_iota(jnp.int32, square, 0) == lax.broadcasted_iota(
        jnp.int32, square, 1
    )
    bias = jnp.sum(jnp.where(diagonal, bias_ref[...], 0.0), axis=1, keepdims=True)
    hidden[...] = jnp.broadcast_to(bias, hidden.shape)
    mix = jnp.concatenate(
        [jnp.concatenate([weight_ref[3 * a + b] for b in range(3)], axis=1) for a in range(3)],
        axis=0,
    )
    for j in range(Y // 2):
        at = j * 2 * X
        part = jnp.dot(mix, stack[:, at : at + 2 * X], preferred_element_type=jnp.float32)
        for a in range(3):
            place = slice(at + (2 - a) * X, at + (4 - a) * X)
            hidden[:, place] += part[a * C : (a + 1) * C]
    for y in range(Y):
        h = hidden[:, (y + 1) * X : (y + 2) * X]
        s = jax.nn.sigmoid(h)
        slope_ref[y] = s * (1.0 + h * (1.0 - s))


def weight_kernel(g_ref, slope_ref, turned_ref, grad_ref, sums_ref, stack):
    zero = jnp.zeros((C, X), jnp.bfloat16)
    stack[0:C, (Y - 1) * X :] = zero
    stack[2 * C :, 0:X] = zero
    for y in range(Y):
        grad = (g_ref[PLACE[y]].astype(jnp.float32) * slope_ref[y]).astype(jnp.bfloat16)
        grad_ref[y] = grad
        for a in range(3):
            row = y + a - 1
            if 0 <= row < Y:
                stack[a * C : (a + 1) * C, row * X : (row + 1) * X] = grad
    total = jnp.zeros((3 * C, WIDE), jnp.float32)
    for j in range(Y // 2):
        at = slice(j * 2 * X, (j + 1) * 2 * X)
        total += jnp.dot(stack[:, at], turned_ref[at, :], preferred_element_type=jnp.float32)
    square = (C, C)
    diagonal = lax.broadcasted_iota(jnp.int32, square, 0) == lax.broadcasted_iota(
        jnp.int32, square, 1
    )
    bias = total[C : 2 * C, 3 * C : 3 * C + 1]
    row = jnp.sum(jnp.where(diagonal, bias, 0.0), axis=0, keepdims=True)
    first = lax.broadcasted_iota(jnp.int32, square, 0) == 0
    last = jnp.where(first, row, 0.0)
    blocks = [
        total[a * C : (a + 1) * C, b * C : (b + 1) * C] for a in range(3) for b in range(3)
    ]
    whole = jnp.concatenate(blocks + [last], axis=1)
    for piece in range(N_FLAT):
        sums_ref[piece] = whole[piece * PIECE : (piece + 1) * PIECE]


def input_kernel(grad_ref, g_ref, weight_ref, out_ref, stack, total):
    total[...] = jnp.zeros_like(total)
    for y in range(Y):
        row = grad_ref[y].astype(jnp.float32)
        whole = jnp.concatenate([shifted(row, 1 - b) for b in range(3)], axis=0)
        stack[:, y * X : (y + 1) * X] = whole.astype(jnp.bfloat16)
    mix = jnp.concatenate(
        [
            jnp.concatenate(
                [weight_ref[3 * a + b].astype(jnp.float32).T for b in range(3)], axis=1
            )
            for a in range(3)
        ],
        axis=0,
    ).astype(jnp.bfloat16)
    for j in range(Y // 2):
        at = j * 2 * X
        part = jnp.dot(mix, stack[:, at : at + 2 * X], preferred_element_type=jnp.float32)
        for a in range(3):
            place = slice(at + a * X, at + (a + 2) * X)
            total[:, place] += part[a * C : (a + 1) * C]
    for y in range(0, Y, 16):
        rows = []
        for row in range(y, y + 16):
            conv = total[:, (row + 1) * X : (row + 2) * X]
            rows.append(g_ref[PLACE[row]].astype(jnp.float32) + conv)
        turned = jnp.swapaxes(jnp.stack(rows), 0, 1)
        out_ref[:, y : y + 16] = turned.astype(jnp.bfloat16)


def turn_kernel(own_ref, other_ref, rows_ref, last_ref):
    for slot, raw_ref in enumerate((own_ref, other_ref)):
        rows = jnp.swapaxes(raw_ref[...].astype(jnp.float32), 0, 1).astype(jnp.bfloat16)
        rows_ref[slot] = rows
        last_ref[slot] = rows[3]


def blur_kernel(half_ref, taps_ref, rows_ref, halo_ref, out_ref):
    half = half_ref[0]
    for slot, place in enumerate((half, 1 - half)):
        before = halo_ref[slot].astype(jnp.float32)
        for k in range(4):
            row = rows_ref[slot, k].astype(jnp.float32)
            for pair in range(4):
                value = taps_ref[pair : pair + 1] * row
                if pair == 0:
                    value = value + taps_ref[4:5] * before
                out_ref[CROSS_ORDER.index((k, pair)), place] = value.astype(jnp.bfloat16)
            before = row


def unpack_kernel(whole_ref, weight_ref, bias_ref):
    whole = jnp.concatenate([whole_ref[piece] for piece in range(N_FLAT)], axis=0)
    for tap in range(9):
        weight_ref[tap] = whole[:, tap * C : (tap + 1) * C]
    bias_ref[...] = whole[0:1, 9 * C :]


def spread_sum_kernel(parts_ref, out_ref):
    total = jnp.sum(parts_ref[...], axis=0)
    for copy in range(out_ref.shape[0]):
        out_ref[copy] = total


def scaled_sum_kernel(factor, parts_ref, out_ref):
    total = jnp.sum(parts_ref[...], axis=0) * factor
    for copy in range(out_ref.shape[0]):
        out_ref[copy] = total


def call(kernel, outs, scratch, flops, moved, *args, scalars=0, far=0):
    return pl.pallas_call(
        kernel,
        out_shape=outs,
        in_specs=[pl.BlockSpec(memory_space=pltpu.SMEM)] * scalars
        + [pl.BlockSpec(memory_space=pltpu.VMEM)] * (len(args) - scalars - far)
        + [pl.BlockSpec(memory_space=pltpu.HBM)] * far,
        out_specs=jax.tree.map(lambda _: pl.BlockSpec(memory_space=pltpu.VMEM), outs),
        scratch_shapes=scratch,
        compiler_params=pltpu.CompilerParams(vmem_limit_bytes=VMEM_LIMIT),
        cost_estimate=pl.CostEstimate(flops=flops, bytes_accessed=moved, transcendentals=0),
    )(*args)


def on_device(activations, cotangent, weight, conv_bias, blur_taps):
    shape = jax.ShapeDtypeStruct
    bf16, f32 = jnp.bfloat16, jnp.float32
    raw = cotangent[:, :, 0, :]
    other = lax.ppermute(raw, "zh", [(0, 1), (1, 0)])
    half = lax.axis_index("zh").astype(jnp.int32)[None]
    flops = 2 * Y * X * 9 * C * C
    slope, turned, coef = call(
        forward_kernel,
        (shape((Y, C, X), f32), shape((Y * X, WIDE), bf16), shape((8, X), f32)),
        [
            pltpu.VMEM((3 * C, Y * X), bf16),
            pltpu.VMEM((C, (Y + 2) * X), f32),
            pltpu.VMEM((1, 9), f32),
            pltpu.VMEM((1, C), f32),
            pltpu.VMEM((C, Y, X), bf16),
            pltpu.VMEM((9, C, C), bf16),
            pltpu.SemaphoreType.DMA((4,)),
        ],
        64 * flops,
        128 << 20,
        half,
        *[
            pltpu.with_memory_space_constraint(array, pltpu.HBM)
            for array in (blur_taps[None], conv_bias[None], activations[:, 0], weight)
        ],
        scalars=1,
        far=4,
    )
    slope, turned, coef, raw = lax.optimization_barrier((slope, turned, coef, raw))
    rows, last = call(
        turn_kernel,
        (shape((2, 4, C, X), bf16), shape((2, C, X), bf16)),
        [],
        1 << 16,
        1 << 18,
        raw,
        other,
    )
    hops = [
        ((group * N_CROSS + cross) * 2, ((group + 1) * N_CROSS + cross) * 2)
        for group in range(N_GROUP - 1)
        for cross in range(N_CROSS)
    ]
    halo = lax.ppermute(last, AXES, hops)
    field = call(
        blur_kernel,
        shape((N_CROSS, 2, C, X), bf16),
        [],
        1 << 20,
        1 << 20,
        half,
        coef,
        rows,
        halo,
        scalars=1,
    )
    crosses = [
        [(group * 4 + x) * 8 + y * 2 + zh for x, y in CROSS_ORDER]
        for group in range(N_GROUP)
        for zh in range(2)
    ]
    g_out = lax.all_to_all(field, AXES, 0, 0, axis_index_groups=crosses, tiled=True)
    g_out = g_out.reshape(Y, C, X)
    grad, sums = call(
        weight_kernel,
        (shape((Y, C, X), bf16), shape((N_FLAT, PIECE, LONG), f32)),
        [pltpu.VMEM((3 * C, Y * X), bf16)],
        flops,
        4 << 20,
        g_out,
        slope,
        turned,
    )
    grad_input = call(
        input_kernel,
        shape((C, Y, X), bf16),
        [pltpu.VMEM((3 * C, Y * X), bf16), pltpu.VMEM((C, (Y + 2) * X), f32)],
        flops,
        2 << 20,
        grad,
        g_out,
        weight,
    )

    flats = [
        [((zl * 2 + core) * 4 + x) * 8 + y * 2 + zh for core in range(2) for x, y in CROSS_ORDER]
        for zl in range(8)
        for zh in range(2)
    ]
    parts = lax.all_to_all(sums, AXES, 0, 0, axis_index_groups=flats, tiled=True)
    sent = call(
        spread_sum_kernel, shape((N_COLUMN, PIECE, LONG), f32), [], 1 << 16, 1 << 18, parts
    )
    columns = [
        [
            (((z % 8) * 2 + core) * N_CROSS + cross) * 2 + z // 8
            for z in [(FIRST + step) % N_COLUMN for step in range(N_COLUMN)]
        ]
        for core in range(2)
        for cross in range(N_CROSS)
    ]
    parts = lax.all_to_all(sent, AXES, 0, 0, axis_index_groups=columns, tiled=True)
    parts, grad_input = lax.optimization_barrier((parts, grad_input))
    factor = float(512 * Y * X) ** -0.5
    sent = call(
        lambda a, b: scaled_sum_kernel(factor, a, b),
        shape((N_FLAT, PIECE, LONG), f32),
        [],
        1 << 16,
        1 << 18,
        parts,
    )
    whole = lax.all_to_all(sent, AXES, 0, 0, axis_index_groups=flats, tiled=True)
    grad_w, grad_b = call(
        unpack_kernel, (shape((9, C, C), f32), shape((1, C), f32)), [], 1, 1 << 18, whole
    )
    return grad_input[:, None], grad_w, grad_b.reshape(C)


def solution(mesh):
    fine = Mesh(mesh.devices.reshape(SIZES), AXES)
    in_specs = (P(None, AXES, None, None), P(None, GROUP, PLANE, None), P(), P(), P())
    out_specs = (P(None, AXES, None, None), P(), P())
    return jax.shard_map(
        on_device, mesh=fine, in_specs=in_specs, out_specs=out_specs, check_vma=False
    )
```

```python
import jax
import jax.numpy as jnp
from jax import lax
from jax.experimental import pallas as pl
from jax.experimental.pallas import tpu as pltpu
from jax.sharding import Mesh
from jax.sharding import PartitionSpec as P

R = 8
C = 64
Y = 32
X = 128
AXES = ("zl", "core", "x", "y", "zh")
SIZES = (8, 2, 4, 4, 2)
GROUP = ("zl", "core")
PLANE = ("x", "y", "zh")
N_CROSS = 16
N_FLAT = 32
N_GROUP = 16
N_COLUMN = 16
FIRST = 7
PIECE = 2
LONG = 640
WIDE = 256
VMEM_LIMIT = 16 * 1024 * 1024
CORNER = 3
CROSS_ORDER = [
    ((CORNER + a) % 4, (CORNER + b) % 4) for a in range(4) for b in range(4)
]
PLACE = [CROSS_ORDER.index((y // 8, y // 2 % 4)) * 2 + y % 2 for y in range(Y)]


def shifted(row, step):
    if step == 0:
        return row
    lane = lax.broadcasted_iota(jnp.int32, row.shape, 1)
    edge = 0 if step < 0 else X - 1
    return jnp.where(lane == edge, 0.0, pltpu.roll(row, (-step) % X, 1))


def forward_kernel(
    half_ref,
    taps_far,
    bias_far,
    act_far,
    weight_far,
    slope_ref,
    turned_ref,
    coef_ref,
    stack,
    hidden,
    taps_ref,
    bias_ref,
    act_ref,
    weight_ref,
    sems,
):
    fars = (taps_far, bias_far, act_far, weight_far)
    nears = (taps_ref, bias_ref, act_ref, weight_ref)
    copies = [
        pltpu.make_async_copy(far, near, sems.at[i])
        for i, (far, near) in enumerate(zip(fars, nears))
    ]
    for copy in copies:
        copy.start()
    for copy in copies:
        copy.wait()
    low = half_ref[0] == 0
    for pair in range(4):
        even, odd = (taps_ref[:, 2 * pair + i : 2 * pair + i + 1] for i in range(2))
        coef_ref[pair : pair + 1] = jnp.broadcast_to(jnp.where(low, even, odd), (1, X))
    spill = jnp.where(low, taps_ref[:, R : R + 1], 0.0)
    coef_ref[4:] = jnp.broadcast_to(spill, (4, X))
    column = lax.broadcasted_iota(jnp.int32, (X, WIDE - 3 * C), 1)
    ones = jnp.where(column == 0, 1.0, 0.0).astype(jnp.bfloat16)
    for y in range(Y):
        if y % 16 == 0:
            rows = jnp.swapaxes(act_ref[:, y : y + 16].astype(jnp.float32), 0, 1)
        row = rows[y % 16]
        at = slice(y * X, (y + 1) * X)
        whole = jnp.concatenate([shifted(row, b - 1) for b in range(3)], axis=0)
        stack[:, at] = whole.astype(jnp.bfloat16)
        turned_ref[at, : 3 * C] = whole.T.astype(jnp.bfloat16)
        turned_ref[at, 3 * C :] = ones
    square = (C, C)
    diagonal = lax.broadcasted_iota(jnp.int32, square, 0) == lax.broadcasted_iota(
        jnp.int32, square, 1
    )
    bias = jnp.sum(jnp.where(diagonal, bias_ref[...], 0.0), axis=1, keepdims=True)
    hidden[...] = jnp.broadcast_to(bias, hidden.shape)
    mix = jnp.concatenate(
        [jnp.concatenate([weight_ref[3 * a + b] for b in range(3)], axis=1) for a in range(3)],
        axis=0,
    )
    for j in range(Y // 2):
        at = j * 2 * X
        part = jnp.dot(mix, stack[:, at : at + 2 * X], preferred_element_type=jnp.float32)
        for a in range(3):
            place = slice(at + (2 - a) * X, at + (4 - a) * X)
            hidden[:, place] += part[a * C : (a + 1) * C]
    for y in range(Y):
        h = hidden[:, (y + 1) * X : (y + 2) * X]
        s = jax.nn.sigmoid(h)
        slope_ref[y] = s * (1.0 + h * (1.0 - s))


def weight_kernel(g_ref, slope_ref, turned_ref, grad_ref, sums_ref, stack):
    zero = jnp.zeros((C, X), jnp.bfloat16)
    stack[0:C, (Y - 1) * X :] = zero
    stack[2 * C :, 0:X] = zero
    for y in range(Y):
        grad = (g_ref[PLACE[y]].astype(jnp.float32) * slope_ref[y]).astype(jnp.bfloat16)
        grad_ref[y] = grad
        for a in range(3):
            row = y + a - 1
            if 0 <= row < Y:
                stack[a * C : (a + 1) * C, row * X : (row + 1) * X] = grad
    total = jnp.zeros((3 * C, WIDE), jnp.float32)
    for j in range(Y // 2):
        at = slice(j * 2 * X, (j + 1) * 2 * X)
        total += jnp.dot(stack[:, at], turned_ref[at, :], preferred_element_type=jnp.float32)
    square = (C, C)
    diagonal = lax.broadcasted_iota(jnp.int32, square, 0) == lax.broadcasted_iota(
        jnp.int32, square, 1
    )
    bias = total[C : 2 * C, 3 * C : 3 * C + 1]
    row = jnp.sum(jnp.where(diagonal, bias, 0.0), axis=0, keepdims=True)
    first = lax.broadcasted_iota(jnp.int32, square, 0) == 0
    last = jnp.where(first, row, 0.0)
    blocks = [
        total[a * C : (a + 1) * C, b * C : (b + 1) * C] for a in range(3) for b in range(3)
    ]
    whole = jnp.concatenate(blocks + [last], axis=1)
    for piece in range(N_FLAT):
        sums_ref[piece] = whole[piece * PIECE : (piece + 1) * PIECE]


def input_kernel(grad_ref, g_ref, weight_ref, out_ref, stack, total):
    total[...] = jnp.zeros_like(total)
    for y in range(Y):
        row = grad_ref[y].astype(jnp.float32)
        whole = jnp.concatenate([shifted(row, 1 - b) for b in range(3)], axis=0)
        stack[:, y * X : (y + 1) * X] = whole.astype(jnp.bfloat16)
    mix = jnp.concatenate(
        [
            jnp.concatenate(
                [weight_ref[3 * a + b].astype(jnp.float32).T for b in range(3)], axis=1
            )
            for a in range(3)
        ],
        axis=0,
    ).astype(jnp.bfloat16)
    for j in range(Y // 2):
        at = j * 2 * X
        part = jnp.dot(mix, stack[:, at : at + 2 * X], preferred_element_type=jnp.float32)
        for a in range(3):
            place = slice(at + a * X, at + (a + 2) * X)
            total[:, place] += part[a * C : (a + 1) * C]
    for y in range(0, Y, 16):
        rows = []
        for row in range(y, y + 16):
            conv = total[:, (row + 1) * X : (row + 2) * X]
            rows.append(g_ref[PLACE[row]].astype(jnp.float32) + conv)
        turned = jnp.swapaxes(jnp.stack(rows), 0, 1)
        out_ref[:, y : y + 16] = turned.astype(jnp.bfloat16)


def turn_kernel(own_ref, other_ref, rows_ref, last_ref):
    for slot, raw_ref in enumerate((own_ref, other_ref)):
        rows = jnp.swapaxes(raw_ref[...].astype(jnp.float32), 0, 1).astype(jnp.bfloat16)
        rows_ref[slot] = rows
        last_ref[slot] = rows[3]


def blur_kernel(half_ref, taps_ref, rows_ref, halo_ref, out_ref):
    half = half_ref[0]
    for slot, place in enumerate((half, 1 - half)):
        before = halo_ref[slot].astype(jnp.float32)
        for k in range(4):
            row = rows_ref[slot, k].astype(jnp.float32)
            for pair in range(4):
                value = taps_ref[pair : pair + 1] * row
                if pair == 0:
                    value = value + taps_ref[4:5] * before
                out_ref[CROSS_ORDER.index((k, pair)), place] = value.astype(jnp.bfloat16)
            before = row


def unpack_kernel(whole_ref, weight_ref, bias_ref):
    whole = whole_ref[...].astype(jnp.float32)
    whole = jnp.concatenate([whole[piece] for piece in range(N_FLAT)], axis=0)
    for tap in range(9):
        weight_ref[tap] = whole[:, tap * C : (tap + 1) * C]
    bias_ref[...] = whole[0:1, 9 * C :]


def spread_sum_kernel(parts_ref, out_ref):
    total = jnp.sum(parts_ref[...].astype(jnp.float32), axis=0).astype(out_ref.dtype)
    for copy in range(out_ref.shape[0]):
        out_ref[copy] = total


def scaled_sum_kernel(factor, parts_ref, out_ref):
    total = jnp.sum(parts_ref[...].astype(jnp.float32), axis=0) * factor
    total = total.astype(out_ref.dtype)
    for copy in range(out_ref.shape[0]):
        out_ref[copy] = total


def call(kernel, outs, scratch, flops, moved, *args, scalars=0, far=0):
    return pl.pallas_call(
        kernel,
        out_shape=outs,
        in_specs=[pl.BlockSpec(memory_space=pltpu.SMEM)] * scalars
        + [pl.BlockSpec(memory_space=pltpu.VMEM)] * (len(args) - scalars - far)
        + [pl.BlockSpec(memory_space=pltpu.HBM)] * far,
        out_specs=jax.tree.map(lambda _: pl.BlockSpec(memory_space=pltpu.VMEM), outs),
        scratch_shapes=scratch,
        compiler_params=pltpu.CompilerParams(vmem_limit_bytes=VMEM_LIMIT),
        cost_estimate=pl.CostEstimate(flops=flops, bytes_accessed=moved, transcendentals=0),
    )(*args)


def on_device(activations, cotangent, weight, conv_bias, blur_taps):
    shape = jax.ShapeDtypeStruct
    bf16, f32 = jnp.bfloat16, jnp.float32
    raw = cotangent[:, :, 0, :]
    other = lax.ppermute(raw, "zh", [(0, 1), (1, 0)])
    half = lax.axis_index("zh").astype(jnp.int32)[None]
    flops = 2 * Y * X * 9 * C * C
    slope, turned, coef = call(
        forward_kernel,
        (shape((Y, C, X), f32), shape((Y * X, WIDE), bf16), shape((8, X), f32)),
        [
            pltpu.VMEM((3 * C, Y * X), bf16),
            pltpu.VMEM((C, (Y + 2) * X), f32),
            pltpu.VMEM((1, 9), f32),
            pltpu.VMEM((1, C), f32),
            pltpu.VMEM((C, Y, X), bf16),
            pltpu.VMEM((9, C, C), bf16),
            pltpu.SemaphoreType.DMA((4,)),
        ],
        64 * flops,
        128 << 20,
        half,
        *[
            pltpu.with_memory_space_constraint(array, pltpu.HBM)
            for array in (blur_taps[None], conv_bias[None], activations[:, 0], weight)
        ],
        scalars=1,
        far=4,
    )
    slope, turned, coef, raw = lax.optimization_barrier((slope, turned, coef, raw))
    rows, last = call(
        turn_kernel,
        (shape((2, 4, C, X), bf16), shape((2, C, X), bf16)),
        [],
        1 << 16,
        1 << 18,
        raw,
        other,
    )
    hops = [
        ((group * N_CROSS + cross) * 2, ((group + 1) * N_CROSS + cross) * 2)
        for group in range(N_GROUP - 1)
        for cross in range(N_CROSS)
    ]
    halo = lax.ppermute(last, AXES, hops)
    field = call(
        blur_kernel,
        shape((N_CROSS, 2, C, X), bf16),
        [],
        1 << 20,
        1 << 20,
        half,
        coef,
        rows,
        halo,
        scalars=1,
    )
    crosses = [
        [(group * 4 + x) * 8 + y * 2 + zh for x, y in CROSS_ORDER]
        for group in range(N_GROUP)
        for zh in range(2)
    ]
    g_out = lax.all_to_all(field, AXES, 0, 0, axis_index_groups=crosses, tiled=True)
    g_out = g_out.reshape(Y, C, X)
    grad, sums = call(
        weight_kernel,
        (shape((Y, C, X), bf16), shape((N_FLAT, PIECE, LONG), f32)),
        [pltpu.VMEM((3 * C, Y * X), bf16)],
        flops,
        4 << 20,
        g_out,
        slope,
        turned,
    )
    grad_input = call(
        input_kernel,
        shape((C, Y, X), bf16),
        [pltpu.VMEM((3 * C, Y * X), bf16), pltpu.VMEM((C, (Y + 2) * X), f32)],
        flops,
        2 << 20,
        grad,
        g_out,
        weight,
    )

    flats = [
        [((zl * 2 + core) * 4 + x) * 8 + y * 2 + zh for core in range(2) for x, y in CROSS_ORDER]
        for zl in range(8)
        for zh in range(2)
    ]
    parts = lax.all_to_all(sums, AXES, 0, 0, axis_index_groups=flats, tiled=True)
    sent = call(
        spread_sum_kernel, shape((N_COLUMN, PIECE, LONG), bf16), [], 1 << 16, 1 << 18, parts
    )
    columns = [
        [
            (((z % 8) * 2 + core) * N_CROSS + cross) * 2 + z // 8
            for z in [(FIRST + step) % N_COLUMN for step in range(N_COLUMN)]
        ]
        for core in range(2)
        for cross in range(N_CROSS)
    ]
    parts = lax.all_to_all(sent, AXES, 0, 0, axis_index_groups=columns, tiled=True)
    parts, grad_input = lax.optimization_barrier((parts, grad_input))
    factor = float(512 * Y * X) ** -0.5
    sent = call(
        lambda a, b: scaled_sum_kernel(factor, a, b),
        shape((N_FLAT, PIECE, LONG), bf16),
        [],
        1 << 16,
        1 << 18,
        parts,
    )
    whole = lax.all_to_all(sent, AXES, 0, 0, axis_index_groups=flats, tiled=True)
    grad_w, grad_b = call(
        unpack_kernel, (shape((9, C, C), f32), shape((1, C), f32)), [], 1, 1 << 18, whole
    )
    return grad_input[:, None], grad_w, grad_b.reshape(C)


def solution(mesh):
    fine = Mesh(mesh.devices.reshape(SIZES), AXES)
    in_specs = (P(None, AXES, None, None), P(None, GROUP, PLANE, None), P(), P(), P())
    out_specs = (P(None, AXES, None, None), P(), P())
    return jax.shard_map(
        on_device, mesh=fine, in_specs=in_specs, out_specs=out_specs, check_vma=False
    )
```

```python
import jax
import jax.numpy as jnp
from jax import lax
from jax.experimental import pallas as pl
from jax.experimental.pallas import tpu as pltpu
from jax.sharding import Mesh
from jax.sharding import PartitionSpec as P

R = 8
C = 64
Y = 32
X = 128
AXES = ("zl", "core", "x", "y", "zh")
SIZES = (8, 2, 4, 4, 2)
GROUP = ("zl", "core")
PLANE = ("x", "y", "zh")
N_CROSS = 16
N_FLAT = 32
N_GROUP = 16
N_COLUMN = 16
FIRST = 8
PIECE = 2
LONG = 640
WIDE = 256
VMEM_LIMIT = 16 * 1024 * 1024
def ranks(corner):
    return [((corner[0] + a) % 4, (corner[1] + b) % 4) for a in range(4) for b in range(4)]


CROSS_ORDER = ranks((2, 2))
FLAT_ORDER = ranks((2, 2))
PLACE = [CROSS_ORDER.index((y // 8, y // 2 % 4)) * 2 + y % 2 for y in range(Y)]


def shifted(row, step):
    if step == 0:
        return row
    lane = lax.broadcasted_iota(jnp.int32, row.shape, 1)
    edge = 0 if step < 0 else X - 1
    return jnp.where(lane == edge, 0.0, pltpu.roll(row, (-step) % X, 1))


def forward_kernel(
    half_ref,
    taps_far,
    bias_far,
    act_far,
    weight_far,
    slope_ref,
    turned_ref,
    coef_ref,
    stack,
    hidden,
    taps_ref,
    bias_ref,
    act_ref,
    weight_ref,
    sems,
):
    fars = (taps_far, bias_far, act_far, weight_far)
    nears = (taps_ref, bias_ref, act_ref, weight_ref)
    copies = [
        pltpu.make_async_copy(far, near, sems.at[i])
        for i, (far, near) in enumerate(zip(fars, nears))
    ]
    for copy in copies:
        copy.start()
    for copy in copies:
        copy.wait()
    low = half_ref[0] == 0
    for pair in range(4):
        even, odd = (taps_ref[:, 2 * pair + i : 2 * pair + i + 1] for i in range(2))
        coef_ref[pair : pair + 1] = jnp.broadcast_to(jnp.where(low, even, odd), (1, X))
    spill = jnp.where(low, taps_ref[:, R : R + 1], 0.0)
    coef_ref[4:] = jnp.broadcast_to(spill, (4, X))
    column = lax.broadcasted_iota(jnp.int32, (X, WIDE - 3 * C), 1)
    ones = jnp.where(column == 0, 1.0, 0.0).astype(jnp.bfloat16)
    for y in range(Y):
        if y % 16 == 0:
            rows = jnp.swapaxes(act_ref[:, y : y + 16].astype(jnp.float32), 0, 1)
        row = rows[y % 16]
        at = slice(y * X, (y + 1) * X)
        whole = jnp.concatenate([shifted(row, b - 1) for b in range(3)], axis=0)
        stack[:, at] = whole.astype(jnp.bfloat16)
        turned_ref[at, : 3 * C] = whole.T.astype(jnp.bfloat16)
        turned_ref[at, 3 * C :] = ones
    square = (C, C)
    diagonal = lax.broadcasted_iota(jnp.int32, square, 0) == lax.broadcasted_iota(
        jnp.int32, square, 1
    )
    bias = jnp.sum(jnp.where(diagonal, bias_ref[...], 0.0), axis=1, keepdims=True)
    hidden[...] = jnp.broadcast_to(bias, hidden.shape)
    mix = jnp.concatenate(
        [jnp.concatenate([weight_ref[3 * a + b] for b in range(3)], axis=1) for a in range(3)],
        axis=0,
    )
    for j in range(Y // 2):
        at = j * 2 * X
        part = jnp.dot(mix, stack[:, at : at + 2 * X], preferred_element_type=jnp.float32)
        for a in range(3):
            place = slice(at + (2 - a) * X, at + (4 - a) * X)
            hidden[:, place] += part[a * C : (a + 1) * C]
    for y in range(Y):
        h = hidden[:, (y + 1) * X : (y + 2) * X]
        s = jax.nn.sigmoid(h)
        slope_ref[y] = s * (1.0 + h * (1.0 - s))


def weight_kernel(g_ref, slope_ref, turned_ref, grad_ref, sums_ref, stack):
    zero = jnp.zeros((C, X), jnp.bfloat16)
    stack[0:C, (Y - 1) * X :] = zero
    stack[2 * C :, 0:X] = zero
    for y in range(Y):
        grad = (g_ref[PLACE[y]].astype(jnp.float32) * slope_ref[y]).astype(jnp.bfloat16)
        grad_ref[y] = grad
        for a in range(3):
            row = y + a - 1
            if 0 <= row < Y:
                stack[a * C : (a + 1) * C, row * X : (row + 1) * X] = grad
    total = jnp.zeros((3 * C, WIDE), jnp.float32)
    for j in range(Y // 2):
        at = slice(j * 2 * X, (j + 1) * 2 * X)
        total += jnp.dot(stack[:, at], turned_ref[at, :], preferred_element_type=jnp.float32)
    square = (C, C)
    diagonal = lax.broadcasted_iota(jnp.int32, square, 0) == lax.broadcasted_iota(
        jnp.int32, square, 1
    )
    bias = total[C : 2 * C, 3 * C : 3 * C + 1]
    row = jnp.sum(jnp.where(diagonal, bias, 0.0), axis=0, keepdims=True)
    first = lax.broadcasted_iota(jnp.int32, square, 0) == 0
    last = jnp.where(first, row, 0.0)
    blocks = [
        total[a * C : (a + 1) * C, b * C : (b + 1) * C] for a in range(3) for b in range(3)
    ]
    whole = jnp.concatenate(blocks + [last], axis=1)
    for piece in range(N_FLAT):
        sums_ref[piece] = whole[piece * PIECE : (piece + 1) * PIECE]


def input_kernel(grad_ref, g_ref, weight_ref, out_ref, stack, total):
    total[...] = jnp.zeros_like(total)
    for y in range(Y):
        row = grad_ref[y].astype(jnp.float32)
        whole = jnp.concatenate([shifted(row, 1 - b) for b in range(3)], axis=0)
        stack[:, y * X : (y + 1) * X] = whole.astype(jnp.bfloat16)
    mix = jnp.concatenate(
        [
            jnp.concatenate(
                [weight_ref[3 * a + b].astype(jnp.float32).T for b in range(3)], axis=1
            )
            for a in range(3)
        ],
        axis=0,
    ).astype(jnp.bfloat16)
    for j in range(Y // 2):
        at = j * 2 * X
        part = jnp.dot(mix, stack[:, at : at + 2 * X], preferred_element_type=jnp.float32)
        for a in range(3):
            place = slice(at + a * X, at + (a + 2) * X)
            total[:, place] += part[a * C : (a + 1) * C]
    for y in range(0, Y, 16):
        rows = []
        for row in range(y, y + 16):
            conv = total[:, (row + 1) * X : (row + 2) * X]
            rows.append(g_ref[PLACE[row]].astype(jnp.float32) + conv)
        turned = jnp.swapaxes(jnp.stack(rows), 0, 1)
        out_ref[:, y : y + 16] = turned.astype(jnp.bfloat16)


def turn_kernel(own_ref, other_ref, rows_ref, last_ref):
    for slot, raw_ref in enumerate((own_ref, other_ref)):
        rows = jnp.swapaxes(raw_ref[...].astype(jnp.float32), 0, 1).astype(jnp.bfloat16)
        rows_ref[slot] = rows
        last_ref[slot] = rows[3]


def blur_kernel(half_ref, taps_ref, rows_ref, halo_ref, out_ref):
    half = half_ref[0]
    for slot, place in enumerate((half, 1 - half)):
        before = halo_ref[slot].astype(jnp.float32)
        for k in range(4):
            row = rows_ref[slot, k].astype(jnp.float32)
            for pair in range(4):
                value = taps_ref[pair : pair + 1] * row
                if pair == 0:
                    value = value + taps_ref[4:5] * before
                out_ref[CROSS_ORDER.index((k, pair)), place] = value.astype(jnp.bfloat16)
            before = row


def unpack_kernel(whole_ref, weight_ref, bias_ref):
    whole = whole_ref[...].astype(jnp.float32)
    whole = jnp.concatenate([whole[piece] for piece in range(N_FLAT)], axis=0)
    for tap in range(9):
        weight_ref[tap] = whole[:, tap * C : (tap + 1) * C]
    bias_ref[...] = whole[0:1, 9 * C :]


def spread_sum_kernel(parts_ref, out_ref):
    total = jnp.sum(parts_ref[...].astype(jnp.float32), axis=0).astype(out_ref.dtype)
    for copy in range(out_ref.shape[0]):
        out_ref[copy] = total


def scaled_sum_kernel(factor, parts_ref, out_ref):
    total = jnp.sum(parts_ref[...].astype(jnp.float32), axis=0) * factor
    total = total.astype(out_ref.dtype)
    for copy in range(out_ref.shape[0]):
        out_ref[copy] = total


def call(kernel, outs, scratch, flops, moved, *args, scalars=0, far=0):
    return pl.pallas_call(
        kernel,
        out_shape=outs,
        in_specs=[pl.BlockSpec(memory_space=pltpu.SMEM)] * scalars
        + [pl.BlockSpec(memory_space=pltpu.VMEM)] * (len(args) - scalars - far)
        + [pl.BlockSpec(memory_space=pltpu.HBM)] * far,
        out_specs=jax.tree.map(lambda _: pl.BlockSpec(memory_space=pltpu.VMEM), outs),
        scratch_shapes=scratch,
        compiler_params=pltpu.CompilerParams(vmem_limit_bytes=VMEM_LIMIT),
        cost_estimate=pl.CostEstimate(flops=flops, bytes_accessed=moved, transcendentals=0),
    )(*args)


def on_device(activations, cotangent, weight, conv_bias, blur_taps):
    shape = jax.ShapeDtypeStruct
    bf16, f32 = jnp.bfloat16, jnp.float32
    raw = cotangent[:, :, 0, :]
    other = lax.ppermute(raw, "zh", [(0, 1), (1, 0)])
    half = lax.axis_index("zh").astype(jnp.int32)[None]
    flops = 2 * Y * X * 9 * C * C
    slope, turned, coef = call(
        forward_kernel,
        (shape((Y, C, X), f32), shape((Y * X, WIDE), bf16), shape((8, X), f32)),
        [
            pltpu.VMEM((3 * C, Y * X), bf16),
            pltpu.VMEM((C, (Y + 2) * X), f32),
            pltpu.VMEM((1, 9), f32),
            pltpu.VMEM((1, C), f32),
            pltpu.VMEM((C, Y, X), bf16),
            pltpu.VMEM((9, C, C), bf16),
            pltpu.SemaphoreType.DMA((4,)),
        ],
        64 * flops,
        128 << 20,
        half,
        *[
            pltpu.with_memory_space_constraint(array, pltpu.HBM)
            for array in (blur_taps[None], conv_bias[None], activations[:, 0], weight)
        ],
        scalars=1,
        far=4,
    )
    slope, turned, coef, raw = lax.optimization_barrier((slope, turned, coef, raw))
    rows, last = call(
        turn_kernel,
        (shape((2, 4, C, X), bf16), shape((2, C, X), bf16)),
        [],
        1 << 16,
        1 << 18,
        raw,
        other,
    )
    hops = [
        ((group * N_CROSS + cross) * 2, ((group + 1) * N_CROSS + cross) * 2)
        for group in range(N_GROUP - 1)
        for cross in range(N_CROSS)
    ]
    halo = lax.ppermute(last, AXES, hops)
    field = call(
        blur_kernel,
        shape((N_CROSS, 2, C, X), bf16),
        [],
        1 << 20,
        1 << 20,
        half,
        coef,
        rows,
        halo,
        scalars=1,
    )
    crosses = [
        [(group * 4 + x) * 8 + y * 2 + zh for x, y in CROSS_ORDER]
        for group in range(N_GROUP)
        for zh in range(2)
    ]
    g_out = lax.all_to_all(field, AXES, 0, 0, axis_index_groups=crosses, tiled=True)
    g_out = g_out.reshape(Y, C, X)
    grad, sums = call(
        weight_kernel,
        (shape((Y, C, X), bf16), shape((N_FLAT, PIECE, LONG), f32)),
        [pltpu.VMEM((3 * C, Y * X), bf16)],
        flops,
        4 << 20,
        g_out,
        slope,
        turned,
    )
    grad_input = call(
        input_kernel,
        shape((C, Y, X), bf16),
        [pltpu.VMEM((3 * C, Y * X), bf16), pltpu.VMEM((C, (Y + 2) * X), f32)],
        flops,
        2 << 20,
        grad,
        g_out,
        weight,
    )

    flats = [
        [((zl * 2 + core) * 4 + x) * 8 + y * 2 + zh for core in range(2) for x, y in FLAT_ORDER]
        for zl in range(8)
        for zh in range(2)
    ]
    parts = lax.all_to_all(sums, AXES, 0, 0, axis_index_groups=flats, tiled=True)
    sent = call(
        spread_sum_kernel, shape((N_COLUMN, PIECE, LONG), bf16), [], 1 << 16, 1 << 18, parts
    )
    columns = [
        [
            (((z % 8) * 2 + core) * N_CROSS + cross) * 2 + z // 8
            for z in [(FIRST + step) % N_COLUMN for step in range(N_COLUMN)]
        ]
        for core in range(2)
        for cross in range(N_CROSS)
    ]
    parts = lax.all_to_all(sent, AXES, 0, 0, axis_index_groups=columns, tiled=True)
    parts, grad_input = lax.optimization_barrier((parts, grad_input))
    factor = float(512 * Y * X) ** -0.5
    sent = call(
        lambda a, b: scaled_sum_kernel(factor, a, b),
        shape((N_FLAT, PIECE, LONG), bf16),
        [],
        1 << 16,
        1 << 18,
        parts,
    )
    whole = lax.all_to_all(sent, AXES, 0, 0, axis_index_groups=flats, tiled=True)
    grad_w, grad_b = call(
        unpack_kernel, (shape((9, C, C), f32), shape((1, C), f32)), [], 1, 1 << 18, whole
    )
    return grad_input[:, None], grad_w, grad_b.reshape(C)


def solution(mesh):
    fine = Mesh(mesh.devices.reshape(SIZES), AXES)
    in_specs = (P(None, AXES, None, None), P(None, GROUP, PLANE, None), P(), P(), P())
    out_specs = (P(None, AXES, None, None), P(), P())
    return jax.shard_map(
        on_device, mesh=fine, in_specs=in_specs, out_specs=out_specs, check_vma=False
    )
```

```python
import jax
import jax.numpy as jnp
from jax import lax
from jax.experimental import pallas as pl
from jax.experimental.pallas import tpu as pltpu
from jax.sharding import Mesh
from jax.sharding import PartitionSpec as P

R = 8
C = 64
Y = 32
X = 128
AXES = ("zl", "core", "x", "y", "zh")
SIZES = (8, 2, 4, 4, 2)
GROUP = ("zl", "core")
PLANE = ("x", "y", "zh")
N_CROSS = 16
N_FLAT = 32
N_GROUP = 16
N_COLUMN = 16
FIRST = 8
PIECE = 2
LONG = 640
WIDE = 256
VMEM_LIMIT = 16 * 1024 * 1024
def ranks(corner):
    return [((corner[0] + a) % 4, (corner[1] + b) % 4) for a in range(4) for b in range(4)]


CROSS_ORDER = ranks((2, 2))
FLAT_ORDER = ranks((2, 2))
PLACE = [CROSS_ORDER.index((y // 8, y // 2 % 4)) * 2 + y % 2 for y in range(Y)]


def shifted(row, step):
    if step == 0:
        return row
    lane = lax.broadcasted_iota(jnp.int32, row.shape, 1)
    edge = 0 if step < 0 else X - 1
    return jnp.where(lane == edge, 0.0, pltpu.roll(row, (-step) % X, 1))


def forward_kernel(
    half_ref,
    taps_far,
    bias_far,
    act_far,
    weight_far,
    slope_ref,
    turned_ref,
    coef_ref,
    stack,
    hidden,
    taps_ref,
    bias_ref,
    act_ref,
    weight_ref,
    sems,
):
    fars = (taps_far, bias_far, act_far, weight_far)
    nears = (taps_ref, bias_ref, act_ref, weight_ref)
    copies = [
        pltpu.make_async_copy(far, near, sems.at[i])
        for i, (far, near) in enumerate(zip(fars, nears))
    ]
    for copy in copies:
        copy.start()
    for copy in copies:
        copy.wait()
    low = half_ref[0] == 0
    for pair in range(4):
        even, odd = (taps_ref[:, 2 * pair + i : 2 * pair + i + 1] for i in range(2))
        coef_ref[pair : pair + 1] = jnp.broadcast_to(jnp.where(low, even, odd), (1, X))
    spill = jnp.where(low, taps_ref[:, R : R + 1], 0.0)
    coef_ref[4:] = jnp.broadcast_to(spill, (4, X))
    column = lax.broadcasted_iota(jnp.int32, (X, WIDE - 3 * C), 1)
    ones = jnp.where(column == 0, 1.0, 0.0).astype(jnp.bfloat16)
    for y in range(Y):
        if y % 16 == 0:
            rows = jnp.swapaxes(act_ref[:, y : y + 16].astype(jnp.float32), 0, 1)
        row = rows[y % 16]
        at = slice(y * X, (y + 1) * X)
        whole = jnp.concatenate([shifted(row, b - 1) for b in range(3)], axis=0)
        stack[:, at] = whole.astype(jnp.bfloat16)
        turned_ref[at, : 3 * C] = whole.T.astype(jnp.bfloat16)
        turned_ref[at, 3 * C :] = ones
    square = (C, C)
    diagonal = lax.broadcasted_iota(jnp.int32, square, 0) == lax.broadcasted_iota(
        jnp.int32, square, 1
    )
    bias = jnp.sum(jnp.where(diagonal, bias_ref[...], 0.0), axis=1, keepdims=True)
    hidden[...] = jnp.broadcast_to(bias, hidden.shape)
    mix = jnp.concatenate(
        [jnp.concatenate([weight_ref[3 * a + b] for b in range(3)], axis=1) for a in range(3)],
        axis=0,
    )
    for j in range(Y // 2):
        at = j * 2 * X
        part = jnp.dot(mix, stack[:, at : at + 2 * X], preferred_element_type=jnp.float32)
        for a in range(3):
            place = slice(at + (2 - a) * X, at + (4 - a) * X)
            hidden[:, place] += part[a * C : (a + 1) * C]
    for y in range(Y):
        h = hidden[:, (y + 1) * X : (y + 2) * X]
        s = jax.nn.sigmoid(h)
        slope_ref[y] = s * (1.0 + h * (1.0 - s))


def weight_kernel(g_ref, slope_ref, turned_ref, grad_ref, sums_ref, stack):
    zero = jnp.zeros((C, X), jnp.bfloat16)
    stack[0:C, (Y - 1) * X :] = zero
    stack[2 * C :, 0:X] = zero
    for y in range(Y):
        grad = (g_ref[PLACE[y]].astype(jnp.float32) * slope_ref[y]).astype(jnp.bfloat16)
        grad_ref[y] = grad
        for a in range(3):
            row = y + a - 1
            if 0 <= row < Y:
                stack[a * C : (a + 1) * C, row * X : (row + 1) * X] = grad
    total = jnp.zeros((3 * C, WIDE), jnp.float32)
    for j in range(Y // 2):
        at = slice(j * 2 * X, (j + 1) * 2 * X)
        total += jnp.dot(stack[:, at], turned_ref[at, :], preferred_element_type=jnp.float32)
    square = (C, C)
    diagonal = lax.broadcasted_iota(jnp.int32, square, 0) == lax.broadcasted_iota(
        jnp.int32, square, 1
    )
    bias = total[C : 2 * C, 3 * C : 3 * C + 1]
    row = jnp.sum(jnp.where(diagonal, bias, 0.0), axis=0, keepdims=True)
    first = lax.broadcasted_iota(jnp.int32, square, 0) == 0
    last = jnp.where(first, row, 0.0)
    blocks = [
        total[a * C : (a + 1) * C, b * C : (b + 1) * C] for a in range(3) for b in range(3)
    ]
    whole = jnp.concatenate(blocks + [last], axis=1)
    for piece in range(N_FLAT):
        sums_ref[piece] = whole[piece * PIECE : (piece + 1) * PIECE]


def input_kernel(grad_ref, g_ref, weight_ref, out_ref, stack, total):
    total[...] = jnp.zeros_like(total)
    for y in range(Y):
        row = grad_ref[y].astype(jnp.float32)
        whole = jnp.concatenate([shifted(row, 1 - b) for b in range(3)], axis=0)
        stack[:, y * X : (y + 1) * X] = whole.astype(jnp.bfloat16)
    mix = jnp.concatenate(
        [
            jnp.concatenate(
                [weight_ref[3 * a + b].astype(jnp.float32).T for b in range(3)], axis=1
            )
            for a in range(3)
        ],
        axis=0,
    ).astype(jnp.bfloat16)
    for j in range(Y // 2):
        at = j * 2 * X
        part = jnp.dot(mix, stack[:, at : at + 2 * X], preferred_element_type=jnp.float32)
        for a in range(3):
            place = slice(at + a * X, at + (a + 2) * X)
            total[:, place] += part[a * C : (a + 1) * C]
    for y in range(0, Y, 16):
        rows = []
        for row in range(y, y + 16):
            conv = total[:, (row + 1) * X : (row + 2) * X]
            rows.append(g_ref[PLACE[row]].astype(jnp.float32) + conv)
        turned = jnp.swapaxes(jnp.stack(rows), 0, 1)
        out_ref[:, y : y + 16] = turned.astype(jnp.bfloat16)


def turn_kernel(own_ref, other_ref, rows_ref, last_ref):
    for slot, raw_ref in enumerate((own_ref, other_ref)):
        rows = jnp.swapaxes(raw_ref[...].astype(jnp.float32), 0, 1).astype(jnp.bfloat16)
        rows_ref[slot] = rows
        last_ref[slot] = rows[3]


def blur_kernel(half_ref, taps_ref, rows_ref, halo_ref, out_ref):
    half = half_ref[0]
    for slot, place in enumerate((half, 1 - half)):
        before = halo_ref[slot].astype(jnp.float32)
        for k in range(4):
            row = rows_ref[slot, k].astype(jnp.float32)
            for pair in range(4):
                value = taps_ref[pair : pair + 1] * row
                if pair == 0:
                    value = value + taps_ref[4:5] * before
                out_ref[CROSS_ORDER.index((k, pair)), place] = value.astype(jnp.bfloat16)
            before = row


def unpack_kernel(whole_ref, weight_ref, bias_ref):
    whole = whole_ref[...].astype(jnp.float32)
    whole = jnp.concatenate([whole[piece] for piece in range(N_FLAT)], axis=0)
    for tap in range(9):
        weight_ref[tap] = whole[:, tap * C : (tap + 1) * C]
    bias_ref[...] = whole[0:1, 9 * C :]


def spread_sum_kernel(parts_ref, out_ref):
    total = jnp.sum(parts_ref[...].astype(jnp.float32), axis=0).astype(out_ref.dtype)
    for copy in range(out_ref.shape[0]):
        out_ref[copy] = total


def scaled_sum_kernel(factor, parts_ref, out_ref):
    total = jnp.sum(parts_ref[...].astype(jnp.float32), axis=0) * factor
    total = total.astype(out_ref.dtype)
    for copy in range(out_ref.shape[0]):
        out_ref[copy] = total


def call(kernel, outs, scratch, flops, moved, *args, scalars=0, far=0):
    return pl.pallas_call(
        kernel,
        out_shape=outs,
        in_specs=[pl.BlockSpec(memory_space=pltpu.SMEM)] * scalars
        + [pl.BlockSpec(memory_space=pltpu.VMEM)] * (len(args) - scalars - far)
        + [pl.BlockSpec(memory_space=pltpu.HBM)] * far,
        out_specs=jax.tree.map(lambda _: pl.BlockSpec(memory_space=pltpu.VMEM), outs),
        scratch_shapes=scratch,
        compiler_params=pltpu.CompilerParams(vmem_limit_bytes=VMEM_LIMIT),
        cost_estimate=pl.CostEstimate(flops=flops, bytes_accessed=moved, transcendentals=0),
    )(*args)


def on_device(activations, cotangent, weight, conv_bias, blur_taps):
    shape = jax.ShapeDtypeStruct
    bf16, f32 = jnp.bfloat16, jnp.float32
    raw = cotangent[:, :, 0, :]
    other = lax.ppermute(raw, "zh", [(0, 1), (1, 0)])
    half = lax.axis_index("zh").astype(jnp.int32)[None]
    flops = 2 * Y * X * 9 * C * C
    slope, turned, coef = call(
        forward_kernel,
        (shape((Y, C, X), f32), shape((Y * X, WIDE), bf16), shape((8, X), f32)),
        [
            pltpu.VMEM((3 * C, Y * X), bf16),
            pltpu.VMEM((C, (Y + 2) * X), f32),
            pltpu.VMEM((1, 9), f32),
            pltpu.VMEM((1, C), f32),
            pltpu.VMEM((C, Y, X), bf16),
            pltpu.VMEM((9, C, C), bf16),
            pltpu.SemaphoreType.DMA((4,)),
        ],
        64 * flops,
        128 << 20,
        half,
        *[
            pltpu.with_memory_space_constraint(array, pltpu.HBM)
            for array in (blur_taps[None], conv_bias[None], activations[:, 0], weight)
        ],
        scalars=1,
        far=4,
    )
    slope, turned, coef, raw = lax.optimization_barrier((slope, turned, coef, raw))
    rows, last = call(
        turn_kernel,
        (shape((2, 4, C, X), bf16), shape((2, C, X), bf16)),
        [],
        1 << 16,
        1 << 18,
        raw,
        other,
    )
    hops = [
        ((group * N_CROSS + cross) * 2, ((group + 1) * N_CROSS + cross) * 2)
        for group in range(N_GROUP - 1)
        for cross in range(N_CROSS)
    ]
    halo = lax.ppermute(last, AXES, hops)
    field = call(
        blur_kernel,
        shape((N_CROSS, 2, C, X), bf16),
        [],
        1 << 20,
        1 << 20,
        half,
        coef,
        rows,
        halo,
        scalars=1,
    )
    crosses = [
        [(group * 4 + x) * 8 + y * 2 + zh for x, y in CROSS_ORDER]
        for group in range(N_GROUP)
        for zh in range(2)
    ]
    g_out = lax.all_to_all(field, AXES, 0, 0, axis_index_groups=crosses, tiled=True)
    g_out = g_out.reshape(Y, C, X)
    grad, sums = call(
        weight_kernel,
        (shape((Y, C, X), bf16), shape((N_FLAT, PIECE, LONG), f32)),
        [pltpu.VMEM((3 * C, Y * X), bf16)],
        flops,
        4 << 20,
        g_out,
        slope,
        turned,
    )
    grad_input = call(
        input_kernel,
        shape((C, Y, X), bf16),
        [pltpu.VMEM((3 * C, Y * X), bf16), pltpu.VMEM((C, (Y + 2) * X), f32)],
        flops,
        2 << 20,
        grad,
        g_out,
        weight,
    )

    flats = [
        [((zl * 2 + core) * 4 + x) * 8 + y * 2 + zh for core in (1, 0) for x, y in FLAT_ORDER]
        for zl in range(8)
        for zh in range(2)
    ]
    parts = lax.all_to_all(sums, AXES, 0, 0, axis_index_groups=flats, tiled=True)
    sent = call(
        spread_sum_kernel, shape((N_COLUMN, PIECE, LONG), bf16), [], 1 << 16, 1 << 18, parts
    )
    columns = [
        [
            (((z % 8) * 2 + core) * N_CROSS + cross) * 2 + z // 8
            for z in [(FIRST + step) % N_COLUMN for step in range(N_COLUMN)]
        ]
        for core in range(2)
        for cross in range(N_CROSS)
    ]
    parts = lax.all_to_all(sent, AXES, 0, 0, axis_index_groups=columns, tiled=True)
    parts, grad_input = lax.optimization_barrier((parts, grad_input))
    factor = float(512 * Y * X) ** -0.5
    sent = call(
        lambda a, b: scaled_sum_kernel(factor, a, b),
        shape((N_FLAT, PIECE, LONG), bf16),
        [],
        1 << 16,
        1 << 18,
        parts,
    )
    whole = lax.all_to_all(sent, AXES, 0, 0, axis_index_groups=flats, tiled=True)
    grad_w, grad_b = call(
        unpack_kernel, (shape((9, C, C), f32), shape((1, C), f32)), [], 1, 1 << 18, whole
    )
    return grad_input[:, None], grad_w, grad_b.reshape(C)


def solution(mesh):
    fine = Mesh(mesh.devices.reshape(SIZES), AXES)
    in_specs = (P(None, AXES, None, None), P(None, GROUP, PLANE, None), P(), P(), P())
    out_specs = (P(None, AXES, None, None), P(), P())
    return jax.shard_map(
        on_device, mesh=fine, in_specs=in_specs, out_specs=out_specs, check_vma=False
    )
```

```python
import jax
import jax.numpy as jnp
from jax import lax
from jax.experimental import pallas as pl
from jax.experimental.pallas import tpu as pltpu
from jax.sharding import Mesh
from jax.sharding import PartitionSpec as P

R = 8
C = 64
Y = 32
X = 128
AXES = ("zl", "core", "x", "y", "zh")
SIZES = (8, 2, 4, 4, 2)
GROUP = ("zl", "core")
PLANE = ("x", "y", "zh")
N_CROSS = 16
N_FLAT = 32
N_GROUP = 16
N_COLUMN = 16
FIRST = 8
PIECE = 2
LONG = 640
WIDE = 256
VMEM_LIMIT = 16 * 1024 * 1024
def ranks(corner):
    return [((corner[0] + a) % 4, (corner[1] + b) % 4) for a in range(4) for b in range(4)]


CROSS_ORDER = ranks((2, 2))
FLAT_ORDER = ranks((2, 2))
PLACE = [CROSS_ORDER.index((y // 8, y // 2 % 4)) * 2 + y % 2 for y in range(Y)]


def shifted(row, step):
    if step == 0:
        return row
    lane = lax.broadcasted_iota(jnp.int32, row.shape, 1)
    edge = 0 if step < 0 else X - 1
    return jnp.where(lane == edge, 0.0, pltpu.roll(row, (-step) % X, 1))


def forward_kernel(
    half_ref,
    taps_far,
    bias_far,
    act_far,
    weight_far,
    slope_ref,
    turned_ref,
    coef_ref,
    stack,
    hidden,
    taps_ref,
    bias_ref,
    act_ref,
    weight_ref,
    sems,
):
    fars = (taps_far, bias_far, act_far, weight_far)
    nears = (taps_ref, bias_ref, act_ref, weight_ref)
    copies = [
        pltpu.make_async_copy(far, near, sems.at[i])
        for i, (far, near) in enumerate(zip(fars, nears))
    ]
    for copy in copies:
        copy.start()
    for copy in copies:
        copy.wait()
    low = half_ref[0] == 0
    for pair in range(4):
        even, odd = (taps_ref[:, 2 * pair + i : 2 * pair + i + 1] for i in range(2))
        coef_ref[pair : pair + 1] = jnp.broadcast_to(jnp.where(low, even, odd), (1, X))
    spill = jnp.where(low, taps_ref[:, R : R + 1], 0.0)
    coef_ref[4:] = jnp.broadcast_to(spill, (4, X))
    column = lax.broadcasted_iota(jnp.int32, (X, WIDE - 3 * C), 1)
    ones = jnp.where(column == 0, 1.0, 0.0).astype(jnp.bfloat16)
    for y in range(Y):
        if y % 16 == 0:
            rows = jnp.swapaxes(act_ref[:, y : y + 16].astype(jnp.float32), 0, 1)
        row = rows[y % 16]
        at = slice(y * X, (y + 1) * X)
        whole = jnp.concatenate([shifted(row, b - 1) for b in range(3)], axis=0)
        stack[:, at] = whole.astype(jnp.bfloat16)
        turned_ref[at, : 3 * C] = whole.T.astype(jnp.bfloat16)
        turned_ref[at, 3 * C :] = ones
    square = (C, C)
    diagonal = lax.broadcasted_iota(jnp.int32, square, 0) == lax.broadcasted_iota(
        jnp.int32, square, 1
    )
    bias = jnp.sum(jnp.where(diagonal, bias_ref[...], 0.0), axis=1, keepdims=True)
    hidden[...] = jnp.broadcast_to(bias, hidden.shape)
    mix = jnp.concatenate(
        [jnp.concatenate([weight_ref[3 * a + b] for b in range(3)], axis=1) for a in range(3)],
        axis=0,
    )
    for j in range(Y // 2):
        at = j * 2 * X
        part = jnp.dot(mix, stack[:, at : at + 2 * X], preferred_element_type=jnp.float32)
        for a in range(3):
            place = slice(at + (2 - a) * X, at + (4 - a) * X)
            hidden[:, place] += part[a * C : (a + 1) * C]
    for y in range(Y):
        h = hidden[:, (y + 1) * X : (y + 2) * X]
        s = jax.nn.sigmoid(h)
        slope_ref[y] = s * (1.0 + h * (1.0 - s))


def weight_kernel(g_ref, slope_ref, turned_ref, grad_ref, sums_ref, stack):
    zero = jnp.zeros((C, X), jnp.bfloat16)
    stack[0:C, (Y - 1) * X :] = zero
    stack[2 * C :, 0:X] = zero
    for y in range(Y):
        grad = (g_ref[PLACE[y]].astype(jnp.float32) * slope_ref[y]).astype(jnp.bfloat16)
        grad_ref[y] = grad
        for a in range(3):
            row = y + a - 1
            if 0 <= row < Y:
                stack[a * C : (a + 1) * C, row * X : (row + 1) * X] = grad
    total = jnp.zeros((3 * C, WIDE), jnp.float32)
    for j in range(Y // 2):
        at = slice(j * 2 * X, (j + 1) * 2 * X)
        total += jnp.dot(stack[:, at], turned_ref[at, :], preferred_element_type=jnp.float32)
    square = (C, C)
    diagonal = lax.broadcasted_iota(jnp.int32, square, 0) == lax.broadcasted_iota(
        jnp.int32, square, 1
    )
    bias = total[C : 2 * C, 3 * C : 3 * C + 1]
    row = jnp.sum(jnp.where(diagonal, bias, 0.0), axis=0, keepdims=True)
    first = lax.broadcasted_iota(jnp.int32, square, 0) == 0
    last = jnp.where(first, row, 0.0)
    blocks = [
        total[a * C : (a + 1) * C, b * C : (b + 1) * C] for a in range(3) for b in range(3)
    ]
    whole = jnp.concatenate(blocks + [last], axis=1)
    for piece in range(N_FLAT):
        sums_ref[piece] = whole[piece * PIECE : (piece + 1) * PIECE]


def input_kernel(grad_ref, g_ref, weight_ref, out_ref, stack, total):
    total[...] = jnp.zeros_like(total)
    for y in range(Y):
        row = grad_ref[y].astype(jnp.float32)
        whole = jnp.concatenate([shifted(row, 1 - b) for b in range(3)], axis=0)
        stack[:, y * X : (y + 1) * X] = whole.astype(jnp.bfloat16)
    mix = jnp.concatenate(
        [
            jnp.concatenate(
                [weight_ref[3 * a + b].astype(jnp.float32).T for b in range(3)], axis=1
            )
            for a in range(3)
        ],
        axis=0,
    ).astype(jnp.bfloat16)
    for j in range(Y // 2):
        at = j * 2 * X
        part = jnp.dot(mix, stack[:, at : at + 2 * X], preferred_element_type=jnp.float32)
        for a in range(3):
            place = slice(at + a * X, at + (a + 2) * X)
            total[:, place] += part[a * C : (a + 1) * C]
    for y in range(0, Y, 16):
        rows = []
        for row in range(y, y + 16):
            conv = total[:, (row + 1) * X : (row + 2) * X]
            rows.append(g_ref[PLACE[row]].astype(jnp.float32) + conv)
        turned = jnp.swapaxes(jnp.stack(rows), 0, 1)
        out_ref[:, y : y + 16] = turned.astype(jnp.bfloat16)


def turn_kernel(own_ref, other_ref, rows_ref, last_ref):
    for slot, raw_ref in enumerate((own_ref, other_ref)):
        rows = jnp.swapaxes(raw_ref[...].astype(jnp.float32), 0, 1).astype(jnp.bfloat16)
        rows_ref[slot] = rows
        last_ref[slot] = rows[3]


def blur_kernel(half_ref, taps_ref, rows_ref, halo_ref, out_ref):
    half = half_ref[0]
    for slot, place in enumerate((half, 1 - half)):
        before = halo_ref[slot].astype(jnp.float32)
        for k in range(4):
            row = rows_ref[slot, k].astype(jnp.float32)
            for pair in range(4):
                value = taps_ref[pair : pair + 1] * row
                if pair == 0:
                    value = value + taps_ref[4:5] * before
                out_ref[CROSS_ORDER.index((k, pair)), place] = value.astype(jnp.bfloat16)
            before = row


def unpack_kernel(whole_ref, weight_ref, bias_ref):
    whole = whole_ref[...].astype(jnp.float32)
    whole = jnp.concatenate([whole[piece] for piece in range(N_FLAT)], axis=0)
    for tap in range(9):
        weight_ref[tap] = whole[:, tap * C : (tap + 1) * C]
    bias_ref[...] = whole[0:1, 9 * C :]


def spread_sum_kernel(parts_ref, out_ref):
    total = jnp.sum(parts_ref[...].astype(jnp.float32), axis=0).astype(out_ref.dtype)
    for copy in range(out_ref.shape[0]):
        out_ref[copy] = total


def scaled_sum_kernel(factor, parts_ref, out_ref):
    total = jnp.sum(parts_ref[...].astype(jnp.float32), axis=0) * factor
    total = total.astype(out_ref.dtype)
    for copy in range(out_ref.shape[0]):
        out_ref[copy] = total


def call(kernel, outs, scratch, flops, moved, *args, scalars=0, far=0):
    return pl.pallas_call(
        kernel,
        out_shape=outs,
        in_specs=[pl.BlockSpec(memory_space=pltpu.SMEM)] * scalars
        + [pl.BlockSpec(memory_space=pltpu.VMEM)] * (len(args) - scalars - far)
        + [pl.BlockSpec(memory_space=pltpu.HBM)] * far,
        out_specs=jax.tree.map(lambda _: pl.BlockSpec(memory_space=pltpu.VMEM), outs),
        scratch_shapes=scratch,
        compiler_params=pltpu.CompilerParams(vmem_limit_bytes=VMEM_LIMIT),
        cost_estimate=pl.CostEstimate(flops=flops, bytes_accessed=moved, transcendentals=0),
    )(*args)


def on_device(activations, cotangent, weight, conv_bias, blur_taps):
    shape = jax.ShapeDtypeStruct
    bf16, f32 = jnp.bfloat16, jnp.float32
    raw = cotangent[:, :, 0, :]
    other = lax.ppermute(raw, "zh", [(0, 1), (1, 0)])
    half = lax.axis_index("zh").astype(jnp.int32)[None]
    flops = 2 * Y * X * 9 * C * C
    slope, turned, coef = call(
        forward_kernel,
        (shape((Y, C, X), f32), shape((Y * X, WIDE), bf16), shape((8, X), f32)),
        [
            pltpu.VMEM((3 * C, Y * X), bf16),
            pltpu.VMEM((C, (Y + 2) * X), f32),
            pltpu.VMEM((1, 9), f32),
            pltpu.VMEM((1, C), f32),
            pltpu.VMEM((C, Y, X), bf16),
            pltpu.VMEM((9, C, C), bf16),
            pltpu.SemaphoreType.DMA((4,)),
        ],
        64 * flops,
        128 << 20,
        half,
        *[
            pltpu.with_memory_space_constraint(array, pltpu.HBM)
            for array in (blur_taps[None], conv_bias[None], activations[:, 0], weight)
        ],
        scalars=1,
        far=4,
    )
    slope, turned, coef, raw = lax.optimization_barrier((slope, turned, coef, raw))
    rows, last = call(
        turn_kernel,
        (shape((2, 4, C, X), bf16), shape((2, C, X), bf16)),
        [],
        1 << 16,
        1 << 18,
        raw,
        other,
    )
    hops = [
        ((group * N_CROSS + cross) * 2, ((group + 1) * N_CROSS + cross) * 2)
        for group in range(N_GROUP - 1)
        for cross in range(N_CROSS)
    ]
    halo = lax.ppermute(last, AXES, hops)
    field = call(
        blur_kernel,
        shape((N_CROSS, 2, C, X), bf16),
        [],
        1 << 20,
        1 << 20,
        half,
        coef,
        rows,
        halo,
        scalars=1,
    )
    crosses = [
        [(group * 4 + x) * 8 + y * 2 + zh for x, y in CROSS_ORDER]
        for group in range(N_GROUP)
        for zh in range(2)
    ]
    g_out = lax.all_to_all(field, AXES, 0, 0, axis_index_groups=crosses, tiled=True)
    g_out = g_out.reshape(Y, C, X)
    grad, sums = call(
        weight_kernel,
        (shape((Y, C, X), bf16), shape((N_FLAT, PIECE, LONG), f32)),
        [pltpu.VMEM((3 * C, Y * X), bf16)],
        flops,
        4 << 20,
        g_out,
        slope,
        turned,
    )
    grad_input = call(
        input_kernel,
        shape((C, Y, X), bf16),
        [pltpu.VMEM((3 * C, Y * X), bf16), pltpu.VMEM((C, (Y + 2) * X), f32)],
        flops,
        2 << 20,
        grad,
        g_out,
        weight,
    )

    flats = [
        [((zl * 2 + core) * 4 + x) * 8 + y * 2 + zh for core in (1, 0) for x, y in FLAT_ORDER]
        for zl in range(8)
        for zh in range(2)
    ]
    parts = lax.all_to_all(sums, AXES, 0, 0, axis_index_groups=flats, tiled=True)
    sent = call(
        spread_sum_kernel, shape((N_COLUMN, PIECE, LONG), bf16), [], 1 << 16, 1 << 18, parts
    )
    columns = [
        [
            (((z % 8) * 2 + core) * N_CROSS + cross) * 2 + z // 8
            for z in [(FIRST + 5 * step) % N_COLUMN for step in range(N_COLUMN)]
        ]
        for core in range(2)
        for cross in range(N_CROSS)
    ]
    parts = lax.all_to_all(sent, AXES, 0, 0, axis_index_groups=columns, tiled=True)
    parts, grad_input = lax.optimization_barrier((parts, grad_input))
    factor = float(512 * Y * X) ** -0.5
    sent = call(
        lambda a, b: scaled_sum_kernel(factor, a, b),
        shape((N_FLAT, PIECE, LONG), bf16),
        [],
        1 << 16,
        1 << 18,
        parts,
    )
    whole = lax.all_to_all(sent, AXES, 0, 0, axis_index_groups=flats, tiled=True)
    grad_w, grad_b = call(
        unpack_kernel, (shape((9, C, C), f32), shape((1, C), f32)), [], 1, 1 << 18, whole
    )
    return grad_input[:, None], grad_w, grad_b.reshape(C)


def solution(mesh):
    fine = Mesh(mesh.devices.reshape(SIZES), AXES)
    in_specs = (P(None, AXES, None, None), P(None, GROUP, PLANE, None), P(), P(), P())
    out_specs = (P(None, AXES, None, None), P(), P())
    return jax.shard_map(
        on_device, mesh=fine, in_specs=in_specs, out_specs=out_specs, check_vma=False
    )
```

```python
import jax
import jax.numpy as jnp
from jax import lax
from jax.experimental import pallas as pl
from jax.experimental.pallas import tpu as pltpu
from jax.sharding import Mesh
from jax.sharding import PartitionSpec as P

R = 8
C = 64
Y = 32
X = 128
AXES = ("zl", "core", "x", "y", "zh")
SIZES = (8, 2, 4, 4, 2)
GROUP = ("zl", "core")
PLANE = ("x", "y", "zh")
N_CROSS = 16
N_FLAT = 32
N_GROUP = 16
N_COLUMN = 16
FIRST = 8
PIECE = 2
LONG = 640
WIDE = 256
VMEM_LIMIT = 16 * 1024 * 1024
def ranks(corner):
    return [((corner[0] + a) % 4, (corner[1] + b) % 4) for a in range(4) for b in range(4)]


CROSS_ORDER = ranks((2, 2))
FLAT_ORDER = ranks((2, 2))
PLACE = [CROSS_ORDER.index((y // 8, y // 2 % 4)) * 2 + y % 2 for y in range(Y)]


def shifted(row, step):
    if step == 0:
        return row
    lane = lax.broadcasted_iota(jnp.int32, row.shape, 1)
    edge = 0 if step < 0 else X - 1
    return jnp.where(lane == edge, 0.0, pltpu.roll(row, (-step) % X, 1))


def forward_kernel(
    half_ref,
    taps_far,
    bias_far,
    act_far,
    weight_far,
    slope_ref,
    turned_ref,
    coef_ref,
    stack,
    hidden,
    taps_ref,
    bias_ref,
    act_ref,
    weight_ref,
    sems,
):
    fars = (taps_far, bias_far, act_far, weight_far)
    nears = (taps_ref, bias_ref, act_ref, weight_ref)
    copies = [
        pltpu.make_async_copy(far, near, sems.at[i])
        for i, (far, near) in enumerate(zip(fars, nears))
    ]
    for copy in copies:
        copy.start()
    for copy in copies:
        copy.wait()
    low = half_ref[0] == 0
    for pair in range(4):
        even, odd = (taps_ref[:, 2 * pair + i : 2 * pair + i + 1] for i in range(2))
        coef_ref[pair : pair + 1] = jnp.broadcast_to(jnp.where(low, even, odd), (1, X))
    spill = jnp.where(low, taps_ref[:, R : R + 1], 0.0)
    coef_ref[4:] = jnp.broadcast_to(spill, (4, X))
    column = lax.broadcasted_iota(jnp.int32, (X, WIDE - 3 * C), 1)
    ones = jnp.where(column == 0, 1.0, 0.0).astype(jnp.bfloat16)
    for y in range(Y):
        if y % 16 == 0:
            rows = jnp.swapaxes(act_ref[:, y : y + 16].astype(jnp.float32), 0, 1)
        row = rows[y % 16]
        at = slice(y * X, (y + 1) * X)
        whole = jnp.concatenate([shifted(row, b - 1) for b in range(3)], axis=0)
        stack[:, at] = whole.astype(jnp.bfloat16)
        turned_ref[at, : 3 * C] = whole.T.astype(jnp.bfloat16)
        turned_ref[at, 3 * C :] = ones
    square = (C, C)
    diagonal = lax.broadcasted_iota(jnp.int32, square, 0) == lax.broadcasted_iota(
        jnp.int32, square, 1
    )
    bias = jnp.sum(jnp.where(diagonal, bias_ref[...], 0.0), axis=1, keepdims=True)
    hidden[...] = jnp.broadcast_to(bias, hidden.shape)
    mix = jnp.concatenate(
        [jnp.concatenate([weight_ref[3 * a + b] for b in range(3)], axis=1) for a in range(3)],
        axis=0,
    )
    for j in range(Y // 2):
        at = j * 2 * X
        part = jnp.dot(mix, stack[:, at : at + 2 * X], preferred_element_type=jnp.float32)
        for a in range(3):
            place = slice(at + (2 - a) * X, at + (4 - a) * X)
            hidden[:, place] += part[a * C : (a + 1) * C]
    for y in range(Y):
        h = hidden[:, (y + 1) * X : (y + 2) * X]
        s = jax.nn.sigmoid(h)
        slope_ref[y] = s * (1.0 + h * (1.0 - s))


def weight_kernel(g_ref, slope_ref, turned_ref, grad_ref, sums_ref, stack):
    zero = jnp.zeros((C, X), jnp.bfloat16)
    stack[0:C, (Y - 1) * X :] = zero
    stack[2 * C :, 0:X] = zero
    for y in range(Y):
        grad = (g_ref[PLACE[y]].astype(jnp.float32) * slope_ref[y]).astype(jnp.bfloat16)
        grad_ref[y] = grad
        for a in range(3):
            row = y + a - 1
            if 0 <= row < Y:
                stack[a * C : (a + 1) * C, row * X : (row + 1) * X] = grad
    total = jnp.zeros((3 * C, WIDE), jnp.float32)
    for j in range(Y // 2):
        at = slice(j * 2 * X, (j + 1) * 2 * X)
        total += jnp.dot(stack[:, at], turned_ref[at, :], preferred_element_type=jnp.float32)
    square = (C, C)
    diagonal = lax.broadcasted_iota(jnp.int32, square, 0) == lax.broadcasted_iota(
        jnp.int32, square, 1
    )
    bias = total[C : 2 * C, 3 * C : 3 * C + 1]
    row = jnp.sum(jnp.where(diagonal, bias, 0.0), axis=0, keepdims=True)
    first = lax.broadcasted_iota(jnp.int32, square, 0) == 0
    last = jnp.where(first, row, 0.0)
    blocks = [
        total[a * C : (a + 1) * C, b * C : (b + 1) * C] for a in range(3) for b in range(3)
    ]
    whole = jnp.concatenate(blocks + [last], axis=1)
    for piece in range(N_FLAT):
        sums_ref[piece] = whole[piece * PIECE : (piece + 1) * PIECE]


def input_kernel(grad_ref, g_ref, weight_ref, out_ref, stack, total):
    total[...] = jnp.zeros_like(total)
    for y in range(Y):
        row = grad_ref[y].astype(jnp.float32)
        whole = jnp.concatenate([shifted(row, 1 - b) for b in range(3)], axis=0)
        stack[:, y * X : (y + 1) * X] = whole.astype(jnp.bfloat16)
    mix = jnp.concatenate(
        [
            jnp.concatenate(
                [weight_ref[3 * a + b].astype(jnp.float32).T for b in range(3)], axis=1
            )
            for a in range(3)
        ],
        axis=0,
    ).astype(jnp.bfloat16)
    for j in range(Y // 2):
        at = j * 2 * X
        part = jnp.dot(mix, stack[:, at : at + 2 * X], preferred_element_type=jnp.float32)
        for a in range(3):
            place = slice(at + a * X, at + (a + 2) * X)
            total[:, place] += part[a * C : (a + 1) * C]
    for y in range(0, Y, 16):
        rows = []
        for row in range(y, y + 16):
            conv = total[:, (row + 1) * X : (row + 2) * X]
            rows.append(g_ref[PLACE[row]].astype(jnp.float32) + conv)
        turned = jnp.swapaxes(jnp.stack(rows), 0, 1)
        out_ref[:, y : y + 16] = turned.astype(jnp.bfloat16)


def turn_kernel(own_ref, other_ref, rows_ref, last_ref):
    for slot, raw_ref in enumerate((own_ref, other_ref)):
        rows = jnp.swapaxes(raw_ref[...].astype(jnp.float32), 0, 1).astype(jnp.bfloat16)
        rows_ref[slot] = rows
        last_ref[slot] = rows[3]


def blur_kernel(half_ref, taps_ref, rows_ref, halo_ref, out_ref):
    half = half_ref[0]
    for slot, place in enumerate((half, 1 - half)):
        before = halo_ref[slot].astype(jnp.float32)
        for k in range(4):
            row = rows_ref[slot, k].astype(jnp.float32)
            for pair in range(4):
                value = taps_ref[pair : pair + 1] * row
                if pair == 0:
                    value = value + taps_ref[4:5] * before
                out_ref[CROSS_ORDER.index((k, pair)), place] = value.astype(jnp.bfloat16)
            before = row


def unpack_kernel(whole_ref, weight_far, bias_ref, weight_ref, sems):
    whole = whole_ref[...].astype(jnp.float32)
    whole = jnp.concatenate([whole[piece] for piece in range(N_FLAT)], axis=0)
    copies = []
    for tap in range(9):
        weight_ref[tap] = whole[:, tap * C : (tap + 1) * C]
        copy = pltpu.make_async_copy(weight_ref.at[tap], weight_far.at[tap], sems.at[tap])
        copy.start()
        copies.append(copy)
    bias_ref[...] = whole[0:1, 9 * C :]
    for copy in copies:
        copy.wait()


def spread_sum_kernel(parts_ref, out_ref):
    total = jnp.sum(parts_ref[...].astype(jnp.float32), axis=0).astype(out_ref.dtype)
    for copy in range(out_ref.shape[0]):
        out_ref[copy] = total


def scaled_sum_kernel(factor, parts_ref, out_ref):
    total = jnp.sum(parts_ref[...].astype(jnp.float32), axis=0) * factor
    total = total.astype(out_ref.dtype)
    for copy in range(out_ref.shape[0]):
        out_ref[copy] = total


def call(kernel, outs, scratch, flops, moved, *args, scalars=0, far=0):
    return pl.pallas_call(
        kernel,
        out_shape=outs,
        in_specs=[pl.BlockSpec(memory_space=pltpu.SMEM)] * scalars
        + [pl.BlockSpec(memory_space=pltpu.VMEM)] * (len(args) - scalars - far)
        + [pl.BlockSpec(memory_space=pltpu.HBM)] * far,
        out_specs=jax.tree.map(lambda _: pl.BlockSpec(memory_space=pltpu.VMEM), outs),
        scratch_shapes=scratch,
        compiler_params=pltpu.CompilerParams(vmem_limit_bytes=VMEM_LIMIT),
        cost_estimate=pl.CostEstimate(flops=flops, bytes_accessed=moved, transcendentals=0),
    )(*args)


def on_device(activations, cotangent, weight, conv_bias, blur_taps):
    shape = jax.ShapeDtypeStruct
    bf16, f32 = jnp.bfloat16, jnp.float32
    raw = cotangent[:, :, 0, :]
    other = lax.ppermute(raw, "zh", [(0, 1), (1, 0)])
    half = lax.axis_index("zh").astype(jnp.int32)[None]
    flops = 2 * Y * X * 9 * C * C
    slope, turned, coef = call(
        forward_kernel,
        (shape((Y, C, X), f32), shape((Y * X, WIDE), bf16), shape((8, X), f32)),
        [
            pltpu.VMEM((3 * C, Y * X), bf16),
            pltpu.VMEM((C, (Y + 2) * X), f32),
            pltpu.VMEM((1, 9), f32),
            pltpu.VMEM((1, C), f32),
            pltpu.VMEM((C, Y, X), bf16),
            pltpu.VMEM((9, C, C), bf16),
            pltpu.SemaphoreType.DMA((4,)),
        ],
        64 * flops,
        128 << 20,
        half,
        *[
            pltpu.with_memory_space_constraint(array, pltpu.HBM)
            for array in (blur_taps[None], conv_bias[None], activations[:, 0], weight)
        ],
        scalars=1,
        far=4,
    )
    slope, turned, coef, raw = lax.optimization_barrier((slope, turned, coef, raw))
    rows, last = call(
        turn_kernel,
        (shape((2, 4, C, X), bf16), shape((2, C, X), bf16)),
        [],
        1 << 16,
        1 << 18,
        raw,
        other,
    )
    hops = [
        ((group * N_CROSS + cross) * 2, ((group + 1) * N_CROSS + cross) * 2)
        for group in range(N_GROUP - 1)
        for cross in range(N_CROSS)
    ]
    halo = lax.ppermute(last, AXES, hops)
    field = call(
        blur_kernel,
        shape((N_CROSS, 2, C, X), bf16),
        [],
        1 << 20,
        1 << 20,
        half,
        coef,
        rows,
        halo,
        scalars=1,
    )
    crosses = [
        [(group * 4 + x) * 8 + y * 2 + zh for x, y in CROSS_ORDER]
        for group in range(N_GROUP)
        for zh in range(2)
    ]
    g_out = lax.all_to_all(field, AXES, 0, 0, axis_index_groups=crosses, tiled=True)
    g_out = g_out.reshape(Y, C, X)
    grad, sums = call(
        weight_kernel,
        (shape((Y, C, X), bf16), shape((N_FLAT, PIECE, LONG), f32)),
        [pltpu.VMEM((3 * C, Y * X), bf16)],
        flops,
        4 << 20,
        g_out,
        slope,
        turned,
    )
    grad_input = call(
        input_kernel,
        shape((C, Y, X), bf16),
        [pltpu.VMEM((3 * C, Y * X), bf16), pltpu.VMEM((C, (Y + 2) * X), f32)],
        flops,
        2 << 20,
        grad,
        g_out,
        weight,
    )

    flats = [
        [((zl * 2 + core) * 4 + x) * 8 + y * 2 + zh for core in (1, 0) for x, y in FLAT_ORDER]
        for zl in range(8)
        for zh in range(2)
    ]
    parts = lax.all_to_all(sums, AXES, 0, 0, axis_index_groups=flats, tiled=True)
    sent = call(
        spread_sum_kernel, shape((N_COLUMN, PIECE, LONG), bf16), [], 1 << 16, 1 << 18, parts
    )
    columns = [
        [
            (((z % 8) * 2 + core) * N_CROSS + cross) * 2 + z // 8
            for z in [(FIRST + step) % N_COLUMN for step in range(N_COLUMN)]
        ]
        for core in range(2)
        for cross in range(N_CROSS)
    ]
    parts = lax.all_to_all(sent, AXES, 0, 0, axis_index_groups=columns, tiled=True)
    parts, grad_input = lax.optimization_barrier((parts, grad_input))
    factor = float(512 * Y * X) ** -0.5
    sent = call(
        lambda a, b: scaled_sum_kernel(factor, a, b),
        shape((N_FLAT, PIECE, LONG), bf16),
        [],
        1 << 16,
        1 << 18,
        parts,
    )
    whole = lax.all_to_all(sent, AXES, 0, 0, axis_index_groups=flats, tiled=True)
    grad_w, grad_b = pl.pallas_call(
        unpack_kernel,
        out_shape=(shape((9, C, C), f32), shape((1, C), f32)),
        in_specs=[pl.BlockSpec(memory_space=pltpu.VMEM)],
        out_specs=(
            pl.BlockSpec(memory_space=pltpu.HBM),
            pl.BlockSpec(memory_space=pltpu.VMEM),
        ),
        scratch_shapes=[pltpu.VMEM((9, C, C), f32), pltpu.SemaphoreType.DMA((9,))],
        compiler_params=pltpu.CompilerParams(vmem_limit_bytes=VMEM_LIMIT),
    )(whole)
    return grad_input[:, None], grad_w, grad_b.reshape(C)


def solution(mesh):
    fine = Mesh(mesh.devices.reshape(SIZES), AXES)
    in_specs = (P(None, AXES, None, None), P(None, GROUP, PLANE, None), P(), P(), P())
    out_specs = (P(None, AXES, None, None), P(), P())
    return jax.shard_map(
        on_device, mesh=fine, in_specs=in_specs, out_specs=out_specs, check_vma=False
    )
```
